512 devices in a mesh: tm: 128 (over z, y, core), swath: 4 (over x).
Axes of the slice: x: 4, y: 8, z: 8, core: 2. Of those that a mesh axis runs over, the one named last changes fastest.
Arguments:
- design: bfloat16 [128, 2048, 512], P('tm', 'swath'), may hold values from -6 to 6
- process: bfloat16 [128, 512, 512], P('tm', 'swath')
- prior_prec: float32 [128, 512], P('tm', 'swath'), may hold values from 0.05 to 0.5
- routes: int32 [128, 16], P('tm', 'swath'), may hold values from -1 to 127, as said below
- counts: int32 [128, 4], P('tm', 'swath'), may hold values from 1 to 4
Outputs:
- reduced_diag: float32 [128, 512, 512], P('tm', 'swath')
- reduced_coupling: float32 [128, 512, 512], P('tm', 'swath')
The draws below stay inside these ranges and needn't reach their ends.
Inputs may be any that keep to these rules, and one draw needn't show every extreme that they name: `routes`: each value is the holder's own time block i or i + 1, or -1 only where i + 1 would be 128; of one holder's 4 blocks, exactly 2 name i and the others i + 1 or -1.
All inputs are finite; a program needn't handle non-finite values.
Results may differ from the reference program's by a relative error of at most 0.00073.
Values may be sent and summed in bfloat16 or wider, within the bound.
No kernel may reach another device: no remote copies, remote signals or barrier semaphores. Data moves between devices by JAX's collectives and lax.ppermute only.
A program may use at most 64 MiB of HBM per device.

```python
import math
import jax
import jax.numpy as jnp
from jax import lax

B = 512
OBS = 128
CAP = 2
LEVELS = 3
RB = 4
NT = 128
SLOTS = 2048
N_SWATH = 4


def draw_process(key, part):
    first_key, second_key = jax.random.split(jax.random.fold_in(key, 7))
    base = jnp.exp(jax.random.uniform(first_key, (NT, B), jnp.float32, math.log(0.2), math.log(2.0)))
    noise = jax.random.normal(second_key, (NT, B, B), jnp.float32)
    outer = jnp.einsum('tij,tkj->tik', noise, noise, precision=lax.Precision.HIGHEST) / (2.0 * B)
    outer = 0.5 * (outer + jnp.swapaxes(outer, 1, 2))
    matrix = outer + base[:, :, None] * jnp.eye(B, dtype=jnp.float32)[None]
    return matrix.astype(jnp.bfloat16)


def draw_routes(key, part):
    score_key = jax.random.fold_in(key, 11)
    scores = jax.random.randint(score_key, (NT, N_SWATH, RB), 0, 1048576) * RB + jnp.arange(RB, dtype=jnp.int32)
    ranking = jnp.argsort(jnp.argsort(scores, axis=-1), axis=-1)
    ahead = (ranking >= CAP).astype(jnp.int32)
    target = jnp.arange(NT, dtype=jnp.int32)[:, None, None] + ahead
    target = jnp.where(target > NT - 1, -1, target)
    return target.reshape(NT, N_SWATH * RB).astype(jnp.int32)


def draw_counts(key, part):
    first_key, second_key, third_key = jax.random.split(jax.random.fold_in(key, 3), 3)
    values = jax.random.randint(first_key, (NT, N_SWATH), 1, RB + 1)
    row_pick = jax.random.randint(second_key, (), 1, NT)
    col_pick = jax.random.randint(third_key, (), 0, N_SWATH)
    values = values.at[row_pick, col_pick].set(RB)
    values = values.at[row_pick - 1, col_pick].set(RB)
    values = values.at[(row_pick + 1) % NT, col_pick].set(1)
    return values.astype(jnp.int32)


def block_levels(rng, extent, cuts, smallest, largest):
    def one(position, blocks):
        draws = jax.random.uniform(jax.random.fold_in(jax.random.fold_in(rng, 6), position), (blocks,), jnp.float32, smallest / len(cuts), largest / len(cuts))
        return jnp.repeat(jnp.exp(draws), extent[position] // blocks).reshape((-1,) + (1,) * (len(extent) - position - 1))

    factor_of = one(*cuts[0])
    for cut in cuts[1:]:
        factor_of = factor_of * one(*cut)
    return factor_of


def normal_values(own_key, dims, width, most, cuts=(), held_as=jnp.bfloat16):
    result = jax.random.normal(own_key, dims, jnp.float32) * width
    if len(cuts) > 0:
        result = block_levels(own_key, dims, cuts, -0.22, 0.18) * result
    return jnp.clip(result, min=-most, max=most).astype(held_as)


def setup_inputs(seed: int = 0) -> dict:
    seeds = jax.random.split(jax.random.key(seed), 6)
    design = normal_values(seeds[0], (NT, N_SWATH * RB * OBS, B), 1.0, 6.0, ((0, 128), (1, 4)))
    process = draw_process(jax.random.fold_in(seeds[5], 71), 0)
    prior_prec = jnp.clip(jnp.exp(math.log(0.5) - 2.3025851 * jax.random.uniform(seeds[2], (NT, B), jnp.float32) ** block_levels(seeds[2], (NT, B), ((0, 128), (1, 4)), -0.2, 0.2)), 0.05, 0.5)
    routes = draw_routes(jax.random.fold_in(seeds[5], 71), 0)
    counts = draw_counts(jax.random.fold_in(seeds[5], 71), 0)
    return dict(design=design, process=process, prior_prec=prior_prec, routes=routes, counts=counts)


def tri_solve(factor, right):
    return lax.linalg.triangular_solve(factor, right, left_side=True, lower=True)

def reference(design, process, prior_prec, routes, counts):
    raw_rows = design.astype(jnp.float32).reshape(NT, N_SWATH, RB, OBS, B)
    mean_sq = lax.optimization_barrier(jnp.mean(raw_rows * raw_rows, axis=-1, keepdims=True))
    scaled = raw_rows * lax.rsqrt(4.0 * SLOTS * (mean_sq + 1e-06))
    live = jnp.arange(RB)[None, None, :] < counts[:, :, None]
    target = routes.reshape(NT, N_SWATH, RB)
    time_ids = jnp.arange(NT)[:, None, None]
    to_self = live & (target == time_ids)
    to_next = live & (target == time_ids + 1)
    self_rows = jnp.where(to_self[:, :, :, None, None], scaled, 0.0).astype(jnp.bfloat16)
    next_rows = jnp.where(to_next[:, :, :, None, None], scaled, 0.0).astype(jnp.bfloat16)

    def holder_grams(pair):
        own_rows, ahead_rows = pair
        own_rows = own_rows.reshape(-1, B)
        ahead_rows = ahead_rows.reshape(-1, B)
        own_gram = lax.dot_general(own_rows.astype(jnp.float32), own_rows.astype(jnp.float32), (((0,), (0,)), ((), ())), preferred_element_type=jnp.float32)
        ahead_gram = lax.dot_general(ahead_rows.astype(jnp.float32), ahead_rows.astype(jnp.float32), (((0,), (0,)), ((), ())), preferred_element_type=jnp.float32)
        return (own_gram, ahead_gram)
    gram_self, gram_next = lax.map(holder_grams, (self_rows, next_rows))
    zero_block = jnp.zeros((1, B, B), jnp.float32)
    gram = gram_self + jnp.concatenate([zero_block, gram_next[:-1]], axis=0)
    proc = process.astype(jnp.float32)
    previous = jnp.concatenate([zero_block, proc[:-1]], axis=0)
    unit = jnp.eye(B, dtype=jnp.float32)
    diag_blocks = previous + proc + gram + prior_prec[:, :, None] * unit[None]
    coupling = -proc
    for level in range(LEVELS):
        distance = 2 ** level
        factor = jnp.linalg.cholesky(diag_blocks)
        solved = tri_solve(factor, coupling)
        eliminated = jnp.einsum('tji,tjk->tik', solved, solved, precision=lax.Precision.HIGHEST)
        zero_run = jnp.zeros((distance, B, B), jnp.float32)
        left_term = jnp.concatenate([zero_run, eliminated[:-distance]], axis=0)
        unit_run = jnp.broadcast_to(unit, (distance, B, B))
        far_factor = jnp.concatenate([factor[distance:], unit_run], axis=0)
        far_solved = jnp.concatenate([solved[distance:], zero_run], axis=0)
        has_partner = (jnp.arange(NT) + distance < NT)[:, None, None]
        cross = tri_solve(far_factor, jnp.swapaxes(coupling, 1, 2))
        right_term = jnp.einsum('tji,tjk->tik', cross, cross, precision=lax.Precision.HIGHEST)
        new_coupling = jnp.einsum('tji,tjk->tik', cross, far_solved, precision=lax.Precision.HIGHEST)
        diag_blocks = diag_blocks - left_term - jnp.where(has_partner, right_term, 0.0)
        coupling = -new_coupling
    return (diag_blocks, coupling)
```

```python
import functools
import jax
import jax.numpy as jnp
from jax import lax
from jax.experimental import pallas as pl
from jax.experimental.pallas import tpu as pltpu
from jax.sharding import PartitionSpec as P

LEVELS = 3
NB = 128
WIDTH = 16
f32, bf16 = jnp.float32, jnp.bfloat16
VMEM = pl.BlockSpec(memory_space=pltpu.VMEM)
SMEM = pl.BlockSpec(memory_space=pltpu.SMEM)
PARAMS = pltpu.CompilerParams(vmem_limit_bytes=48 * 2**20)
KK, KM, MK = ((0,), (0,)), ((1,), (0,)), ((1,), (1,))


def mm(a, b, dims=KM):
    return lax.dot_general(a, b, (dims, ((), ())), preferred_element_type=f32)


def halves(x):
    high = x.astype(bf16)
    return high, (x - high.astype(f32)).astype(bf16)


def thirds(x):
    high = x.astype(bf16).astype(f32)
    rest = x - high
    mid = rest.astype(bf16).astype(f32)
    return high, mid, rest - mid


def split_dot(a, b, dims=KM):
    return mm(a[0], b[0], dims) + (mm(a[0], b[1], dims) + mm(a[1], b[0], dims))


def block_inverse(a):
    lane = lax.broadcasted_iota(jnp.int32, (WIDTH, NB), 1)
    row = lax.broadcasted_iota(jnp.int32, (WIDTH, NB), 0)
    lane_all = lax.broadcasted_iota(jnp.int32, (NB, NB), 1)
    for start in range(0, NB, WIDTH):
        stop = start + WIDTH
        p = a[start:stop, :]
        inside = (lane >= start) & (lane < stop)
        left = jnp.where(inside, 0.0, jnp.where(lane < start, -p, p))
        h, m, l = thirds(left)
        lhs = jnp.concatenate([h, h, m, h, l, m], axis=0).T.astype(bf16)
        cols = [jnp.broadcast_to(p[:, start + j : start + j + 1], (WIDTH, NB)) for j in range(WIDTH)]
        x = jnp.where(inside, jnp.where(lane - start == row, 1.0, 0.0), p)
        for j in range(WIDTH):
            c = cols[j]
            scale = 1.0 / c[j : j + 1, :]
            here = row == j

            def step(v):
                t = v[j : j + 1, :] * scale
                return jnp.where(here, t, v - c * t)

            for i in range(j + 1, WIDTH):
                cols[i] = step(cols[i])
            x = step(x)
        h, m, l = thirds(x)
        rhs = jnp.concatenate([h, m, h, l, h, m], axis=0).astype(bf16)
        a = jnp.where((lane_all >= start) & (lane_all < stop), 0.0, a) - mm(lhs, rhs)
        rows = [x]
        if start:
            rows = [a[:start]] + rows
        if stop < NB:
            rows = rows + [a[stop:]]
        a = jnp.concatenate(rows, axis=0)
    return a


def inverse_kernel(d_ref, x_ref):
    size = d_ref.shape[0]
    count = size // NB
    x_ref[...] = d_ref[...]
    for b in range(count):
        s = slice(b * NB, (b + 1) * NB)
        inv = block_inverse(x_ref[s, s])
        rows = x_ref[s, :]
        lane = lax.broadcasted_iota(jnp.int32, (NB, size), 1)
        inside = (lane >= b * NB) & (lane < (b + 1) * NB)
        left = jnp.where(lane < b * NB, -rows, rows)
        w = split_dot(halves(inv), halves(jnp.where(inside, 0.0, rows)))
        w = jnp.concatenate([inv if c == b else w[:, c * NB : (c + 1) * NB] for c in range(count)], axis=1)
        w_halves = halves(w)
        for o in [*range(b + 1, count), *range(b)]:
            os = slice(o * NB, (o + 1) * NB)
            kept = [jnp.zeros((NB, NB), f32) if c == b else x_ref[os, c * NB : (c + 1) * NB] for c in range(count)]
            x_ref[os, :] = jnp.concatenate(kept, axis=1) - split_dot(halves(left[:, os].T), w_halves)
        x_ref[s, :] = w


def inverse(d):
    size = d.shape[0]
    return pl.pallas_call(
        inverse_kernel,
        out_shape=jax.ShapeDtypeStruct(d.shape, f32),
        in_specs=[VMEM],
        out_specs=VMEM,
        compiler_params=PARAMS,
        cost_estimate=pl.CostEstimate(flops=60 * size**3, bytes_accessed=8 * size * size, transcendentals=0),
        name="inverse",
    )(d)


def weigh_kernel(total_slots, ids_ref, design_ref, process_ref, own_ref, ahead_ref):
    rows = own_ref.shape[0] // 2
    me, live_count = ids_ref[0], ids_ref[1]
    own_seen = jnp.int32(0)
    for r in range(4):
        target = ids_ref[2 + r]
        is_own = target == me
        live = (r < live_count) & (is_own | (target == me + 1))
        h = design_ref[r * rows : (r + 1) * rows, :].astype(f32)
        mean_sq = jnp.mean(h * h, axis=-1, keepdims=True)
        w = h * lax.rsqrt(4.0 * total_slots * (mean_sq + 1e-06))
        w = jnp.where(live, w, 0.0).astype(bf16)
        ahead_seen = r - own_seen

        @pl.when(is_own)
        def _():
            own_ref[pl.ds(jnp.minimum(own_seen, 1) * rows, rows), :] = w

        @pl.when(jnp.logical_not(is_own))
        def _():
            ahead_ref[pl.ds(jnp.minimum(ahead_seen, 1) * rows, rows), :] = w

        own_seen = own_seen + jnp.where(is_own, 1, 0)
    ahead_ref[2 * rows :, :] = process_ref[...]


def gram_kernel(own_ref, incoming_ref, g_ref):
    both = jnp.concatenate([own_ref[...], incoming_ref[: own_ref.shape[0], :]], axis=0)
    g_ref[...] = mm(both, both, KK)


def products_kernel(sid_ref, x_ref, q0, q1, q2, q3, left_ref, right_ref, a_full, c_full):
    sid = sid_ref[0]
    size = x_ref.shape[0]
    for k, piece in enumerate((q0, q1, q2, q3)):
        at = pl.multiple_of(lax.rem(sid - k + 4, 4) * NB, NB)
        a_full[pl.ds(at, NB), :] = piece[:NB, :].astype(f32)
        c_full[pl.ds(at, NB), :] = piece[NB:, :].astype(f32)
    col = pl.multiple_of(sid * NB, NB)
    lhs = jnp.concatenate([q0[:NB, :].astype(f32), c_full[:, pl.ds(col, NB)].T], axis=0)
    z = split_dot(halves(lhs), halves(x_ref[...]))
    zh, zl = halves(z)
    both = split_dot((zh, zl), halves(c_full[...]))
    right_term = split_dot((zh[:NB], zl[:NB]), halves(a_full[...]), MK)
    coupled = -both[:NB]
    left_ref[:NB, :] = right_term
    left_ref[NB:, :] = coupled
    right_ref[:NB, :] = both[NB:]
    right_ref[NB:, :] = coupled


def products(sid, x, pieces):
    size = x.shape[0]
    out = jax.ShapeDtypeStruct((2 * NB, size), f32)
    return pl.pallas_call(
        products_kernel,
        out_shape=(out, out),
        in_specs=[SMEM] + [VMEM] * 5,
        out_specs=(VMEM, VMEM),
        scratch_shapes=[pltpu.VMEM((size, size), f32)] * 2,
        compiler_params=PARAMS,
        cost_estimate=pl.CostEstimate(flops=4 * size**3, bytes_accessed=16 * size * size, transcendentals=0),
        name="products",
    )(sid, x, *pieces)


def passed_along(block, axis, distance, around=False):
    count = lax.axis_size(axis)
    route = [(i, (i + distance) % count) for i in range(count) if around or 0 <= i + distance < count]
    return lax.ppermute(block, axis, route)


def gathered(rows):
    copies = jnp.concatenate([rows] * lax.axis_size("swath"), axis=0)
    return lax.all_to_all(copies, "swath", 0, 0, tiled=True)


def shards(design, process, prior_prec, routes, counts):
    row_count, size = process.shape[1:]
    me = lax.axis_index("tm")
    sid = lax.axis_index("swath")
    total_slots = design.shape[1] * lax.axis_size("swath")
    ids = jnp.concatenate([me[None].astype(jnp.int32), counts[0], routes[0]])
    half = design.shape[1] // 2
    own, ahead = pl.pallas_call(
        functools.partial(weigh_kernel, total_slots),
        out_shape=(
            jax.ShapeDtypeStruct((half, size), bf16),
            jax.ShapeDtypeStruct((half + row_count, size), bf16),
        ),
        in_specs=[SMEM, VMEM, VMEM],
        out_specs=(VMEM, VMEM),
        compiler_params=PARAMS,
        name="weigh",
    )(ids, design[0], process[0])
    incoming = passed_along(ahead, "tm", 1)
    partial = pl.pallas_call(
        gram_kernel,
        out_shape=jax.ShapeDtypeStruct((size, size), f32),
        in_specs=[VMEM, VMEM],
        out_specs=VMEM,
        compiler_params=PARAMS,
        name="gram",
    )(own, incoming)
    pieces_of_gram = lax.all_to_all(partial, "swath", 0, 0, tiled=True)
    gram = jnp.sum(pieces_of_gram.reshape(-1, row_count, size), axis=0)
    previous = incoming[half:]
    unit_rows = jnp.arange(size)[None, :] == jnp.arange(row_count)[:, None] + sid * row_count
    diag_rows = previous.astype(f32) + process[0].astype(f32) + gram
    diag_rows = diag_rows + jnp.where(unit_rows, prior_prec[0][:, None], 0.0)
    pair = -jnp.concatenate([previous, process[0]], axis=0)
    sids = sid[None].astype(jnp.int32)
    for level in range(LEVELS):
        distance = 2**level
        pieces = [pair] + [passed_along(pair, "swath", k, True) for k in (1, 2, 3)]
        x = inverse(gathered(diag_rows))
        left, right = products(sids, x, pieces)
        from_right = passed_along(left, "tm", -distance)
        from_left = passed_along(right, "tm", distance)
        diag_rows = diag_rows - from_left[:row_count] - from_right[:row_count]
        pair = jnp.concatenate([from_left[row_count:], from_right[row_count:]], axis=0)
    return (diag_rows[None], pair[row_count:][None])


def solution(mesh):
    return jax.shard_map(
        shards,
        mesh=mesh,
        in_specs=(
            P("tm", "swath", None),
            P("tm", "swath", None),
            P("tm", "swath"),
            P("tm", "swath"),
            P("tm", "swath"),
        ),
        out_specs=(P("tm", "swath", None), P("tm", "swath", None)),
        check_vma=False,
    )
```

```python
import functools
import jax
import jax.numpy as jnp
from jax import lax
from jax.experimental import pallas as pl
from jax.experimental.pallas import tpu as pltpu
from jax.sharding import PartitionSpec as P

LEVELS = 3
NB = 128
WIDTH = 16
EXTRA = 16
f32, bf16 = jnp.float32, jnp.bfloat16
VMEM = pl.BlockSpec(memory_space=pltpu.VMEM)
SMEM = pl.BlockSpec(memory_space=pltpu.SMEM)
PARAMS = pltpu.CompilerParams(vmem_limit_bytes=48 * 2**20)
KK, KM, MK = ((0,), (0,)), ((1,), (0,)), ((1,), (1,))


def mm(a, b, dims=KM):
    return lax.dot_general(a, b, (dims, ((), ())), preferred_element_type=f32)


def halves(x):
    high = x.astype(bf16)
    return high, (x - high.astype(f32)).astype(bf16)


def thirds(x):
    high = x.astype(bf16).astype(f32)
    rest = x - high
    mid = rest.astype(bf16).astype(f32)
    return high, mid, rest - mid


def split_dot(a, b, dims=KM):
    return mm(a[0], b[0], dims) + (mm(a[0], b[1], dims) + mm(a[1], b[0], dims))


def block_inverse(a):
    lane = lax.broadcasted_iota(jnp.int32, (WIDTH, NB), 1)
    row = lax.broadcasted_iota(jnp.int32, (WIDTH, NB), 0)
    lane_all = lax.broadcasted_iota(jnp.int32, (NB, NB), 1)
    for start in range(0, NB, WIDTH):
        stop = start + WIDTH
        p = a[start:stop, :]
        inside = (lane >= start) & (lane < stop)
        left = jnp.where(inside, 0.0, jnp.where(lane < start, -p, p))
        h, m, l = thirds(left)
        lhs = jnp.concatenate([h, h, m, h, l, m], axis=0).T.astype(bf16)
        cols = [jnp.broadcast_to(p[:, start + j : start + j + 1], (WIDTH, NB)) for j in range(WIDTH)]
        x = jnp.where(inside, jnp.where(lane - start == row, 1.0, 0.0), p)
        for j in range(WIDTH):
            c = cols[j]
            scale = 1.0 / c[j : j + 1, :]
            here = row == j

            def step(v):
                t = v[j : j + 1, :] * scale
                return jnp.where(here, t, v - c * t)

            for i in range(j + 1, WIDTH):
                cols[i] = step(cols[i])
            x = step(x)
        h, m, l = thirds(x)
        rhs = jnp.concatenate([h, m, h, l, h, m], axis=0).astype(bf16)
        a = jnp.where((lane_all >= start) & (lane_all < stop), 0.0, a) - mm(lhs, rhs)
        rows = [x]
        if start:
            rows = [a[:start]] + rows
        if stop < NB:
            rows = rows + [a[stop:]]
        a = jnp.concatenate(rows, axis=0)
    return a


def inverse_kernel(d_ref, x_ref):
    size = d_ref.shape[0]
    count = size // NB
    x_ref[...] = d_ref[...]
    for b in range(count):
        s = slice(b * NB, (b + 1) * NB)
        inv = block_inverse(x_ref[s, s])
        rows = x_ref[s, :]
        lane = lax.broadcasted_iota(jnp.int32, (NB, size), 1)
        inside = (lane >= b * NB) & (lane < (b + 1) * NB)
        left = jnp.where(lane < b * NB, -rows, rows)
        w = split_dot(halves(inv), halves(jnp.where(inside, 0.0, rows)))
        w = jnp.concatenate([inv if c == b else w[:, c * NB : (c + 1) * NB] for c in range(count)], axis=1)
        w_halves = halves(w)
        for o in [*range(b + 1, count), *range(b)]:
            os = slice(o * NB, (o + 1) * NB)
            kept = [jnp.zeros((NB, NB), f32) if c == b else x_ref[os, c * NB : (c + 1) * NB] for c in range(count)]
            x_ref[os, :] = jnp.concatenate(kept, axis=1) - split_dot(halves(left[:, os].T), w_halves)
        x_ref[s, :] = w


def inverse(d):
    size = d.shape[0]
    return pl.pallas_call(
        inverse_kernel,
        out_shape=jax.ShapeDtypeStruct(d.shape, f32),
        in_specs=[VMEM],
        out_specs=VMEM,
        compiler_params=PARAMS,
        cost_estimate=pl.CostEstimate(flops=60 * size**3, bytes_accessed=8 * size * size, transcendentals=0),
        name="inverse",
    )(d)


def weigh_kernel(total_slots, ids_ref, design_ref, process_ref, prior_ref, own_ref, ahead_ref):
    rows = ahead_ref.shape[0] // 2
    me, live_count = ids_ref[0], ids_ref[1]
    own_seen = jnp.int32(0)
    for r in range(4):
        target = ids_ref[2 + r]
        is_own = target == me
        live = (r < live_count) & (is_own | (target == me + 1))
        h = design_ref[r * rows : (r + 1) * rows, :].astype(f32)
        mean_sq = jnp.mean(h * h, axis=-1, keepdims=True)
        w = h * lax.rsqrt(4.0 * total_slots * (mean_sq + 1e-06))
        w = jnp.where(live, w, 0.0).astype(bf16)
        ahead_seen = r - own_seen

        @pl.when(is_own)
        def _():
            at = jnp.minimum(own_seen, 1) * rows
            for k in range(4):
                own_ref[k, pl.ds(at, rows), :] = w

        @pl.when(jnp.logical_not(is_own))
        def _():
            ahead_ref[pl.ds(jnp.minimum(ahead_seen, 1) * rows, rows), :] = w

        own_seen = own_seen + jnp.where(is_own, 1, 0)
    high, mid, low = thirds(prior_ref[...])
    row = lax.broadcasted_iota(jnp.int32, (EXTRA, prior_ref.shape[1]), 0)
    coded = jnp.where(row == 0, high, jnp.where(row == 1, mid, jnp.where(row == 2, low, 0.0))).astype(bf16)
    coded = jnp.concatenate([coded] * 4, axis=1)
    for k in range(4):
        own_ref[k, 2 * rows : 3 * rows, :] = process_ref[...]
        own_ref[k, 3 * rows :, :] = coded


def start_diag_kernel(own_ref, d_ref, p_ref):
    rows = jnp.concatenate([own_ref[k, : 2 * NB, :] for k in range(4)], axis=0)
    d_ref[...] = mm(rows, rows, KK)
    unit = lax.broadcasted_iota(jnp.int32, (NB, NB), 0) == lax.broadcasted_iota(jnp.int32, (NB, NB), 1)
    for k in range(4):
        s = slice(k * NB, (k + 1) * NB)
        process = own_ref[k, 2 * NB : 3 * NB, :]
        p_ref[s, :] = process
        coded = own_ref[k, 3 * NB :, :NB].astype(f32)
        prior = coded[0:1] + coded[1:2] + coded[2:3]
        d_ref[s, :] += process.astype(f32)
        d_ref[s, s] += jnp.where(unit, prior, 0.0)


def end_diag_kernel(d_in, incoming_ref, previous_ref, d_ref):
    rows = incoming_ref[...]
    d_ref[...] = d_in[...] + previous_ref[...].astype(f32) + mm(rows, rows, KK)


def terms_kernel(with_coupling, sid_ref, x_ref, a_ref, c_ref, *outs):
    col = pl.multiple_of(sid_ref[0] * NB, NB)
    lhs = jnp.concatenate([a_ref[pl.ds(col, NB), :].astype(f32), c_ref[:, pl.ds(col, NB)].astype(f32).T], axis=0)
    z = halves(split_dot(halves(lhs), halves(x_ref[...])))
    top, low = (z[0][:NB], z[1][:NB]), (z[0][NB:], z[1][NB:])
    outs[0][...] = cross_dot(top, a_ref[...], MK)
    if with_coupling:
        both = cross_dot(z, c_ref[...])
        outs[1][...] = both[NB:]
        outs[2][...] = -both[:NB]
    else:
        outs[1][...] = cross_dot(low, c_ref[...])


def cross_dot(a, b, dims=KM):
    if b.dtype == bf16:
        return mm(a[0], b, dims) + mm(a[1], b, dims)
    return split_dot(a, halves(b), dims)


def terms(sid, x, a, c, with_coupling):
    size = x.shape[0]
    out = jax.ShapeDtypeStruct((NB, size), f32)
    count = 3 if with_coupling else 2
    return pl.pallas_call(
        functools.partial(terms_kernel, with_coupling),
        out_shape=(out,) * count,
        in_specs=[SMEM] + [VMEM] * 3,
        out_specs=(VMEM,) * count,
        compiler_params=PARAMS,
        cost_estimate=pl.CostEstimate(flops=4 * size**3, bytes_accessed=16 * size * size, transcendentals=0),
        name="terms",
    )(sid, x, a, c)


def coupling_kernel(x_ref, a_ref, c_ref, n_ref):
    x = halves(x_ref[...])
    if a_ref.dtype == bf16:
        z = mm(a_ref[...], x[0]) + mm(a_ref[...], x[1])
    else:
        z = split_dot(halves(a_ref[...]), x)
    n_ref[...] = -cross_dot(halves(z), c_ref[...])


def coupled(x, a, c):
    size = x.shape[0]
    return pl.pallas_call(
        coupling_kernel,
        out_shape=jax.ShapeDtypeStruct(x.shape, f32),
        in_specs=[VMEM] * 3,
        out_specs=VMEM,
        compiler_params=PARAMS,
        cost_estimate=pl.CostEstimate(flops=12 * size**3, bytes_accessed=16 * size * size, transcendentals=0),
        name="coupling",
    )(x, a, c)


def passed_along(block, axis, distance, around=False):
    count = lax.axis_size(axis)
    route = [(i, (i + distance) % count) for i in range(count) if around or 0 <= i + distance < count]
    return lax.ppermute(block, axis, route)


def gathered(rows):
    copies = jnp.concatenate([rows] * lax.axis_size("swath"), axis=0)
    return lax.all_to_all(copies, "swath", 0, 0, tiled=True)


def shards(design, process, prior_prec, routes, counts):
    row_count, size = process.shape[1:]
    swaths = lax.axis_size("swath")
    me = lax.axis_index("tm")
    sid = lax.axis_index("swath")
    total_slots = design.shape[1] * swaths
    ids = jnp.concatenate([me[None].astype(jnp.int32), counts[0], routes[0]])
    half = design.shape[1] // 2
    payload, ahead = pl.pallas_call(
        functools.partial(weigh_kernel, total_slots),
        out_shape=(
            jax.ShapeDtypeStruct((swaths, half + row_count + EXTRA, size), bf16),
            jax.ShapeDtypeStruct((half, size), bf16),
        ),
        in_specs=[SMEM] + [VMEM] * 3,
        out_specs=(VMEM, VMEM),
        compiler_params=PARAMS,
        name="weigh",
    )(ids, design[0], process[0], prior_prec)
    incoming = passed_along(ahead, "tm", 1)
    own_all = lax.all_to_all(payload, "swath", 0, 0, tiled=True)
    incoming_all = gathered(incoming)
    diag, process_all = pl.pallas_call(
        start_diag_kernel,
        out_shape=(jax.ShapeDtypeStruct((size, size), f32), jax.ShapeDtypeStruct((size, size), bf16)),
        in_specs=[VMEM],
        out_specs=(VMEM, VMEM),
        compiler_params=PARAMS,
        cost_estimate=pl.CostEstimate(flops=2 * 1024 * size**2, bytes_accessed=3 * 2**20, transcendentals=0),
        name="start_diag",
    )(own_all)
    previous_all = passed_along(process_all, "tm", 1)
    diag = pl.pallas_call(
        end_diag_kernel,
        out_shape=jax.ShapeDtypeStruct((size, size), f32),
        in_specs=[VMEM] * 3,
        out_specs=VMEM,
        compiler_params=PARAMS,
        name="end_diag",
    )(diag, incoming_all, previous_all)
    sids = sid[None].astype(jnp.int32)
    rows = lax.dynamic_slice_in_dim(diag, sid * row_count, row_count, 0)
    x = inverse(diag)
    a, c = -previous_all, -process_all
    for level in range(LEVELS):
        distance = 2**level
        last = level == LEVELS - 1
        out = terms(sids, x, a, c, last)
        from_right = passed_along(out[0], "tm", -distance)
        from_left = passed_along(out[1], "tm", distance)
        if last:
            coupling = passed_along(out[2], "tm", -distance)
            return ((rows - from_left - from_right)[None], coupling[None])
        n = coupled(x, a, c)
        rows = rows - from_left - from_right
        x = inverse(gathered(rows))
        a = passed_along(n, "tm", distance)
        c = passed_along(n, "tm", -distance)


def solution(mesh):
    return jax.shard_map(
        shards,
        mesh=mesh,
        in_specs=(
            P("tm", "swath", None),
            P("tm", "swath", None),
            P("tm", "swath"),
            P("tm", "swath"),
            P("tm", "swath"),
        ),
        out_specs=(P("tm", "swath", None), P("tm", "swath", None)),
        check_vma=False,
    )
```

```python
import functools
import jax
import jax.numpy as jnp
from jax import lax
from jax.experimental import pallas as pl
from jax.experimental.pallas import tpu as pltpu
from jax.sharding import PartitionSpec as P

LEVELS = 3
NB = 128
WIDTH = 16
HALF = NB // 2
f32, bf16 = jnp.float32, jnp.bfloat16
VMEM = pl.BlockSpec(memory_space=pltpu.VMEM)
SMEM = pl.BlockSpec(memory_space=pltpu.SMEM)
PARAMS = pltpu.CompilerParams(vmem_limit_bytes=48 * 2**20)
KK, KM, MK = ((0,), (0,)), ((1,), (0,)), ((1,), (1,))


def mm(a, b, dims=KM):
    return lax.dot_general(a, b, (dims, ((), ())), preferred_element_type=f32)


def halves(x):
    high = x.astype(bf16)
    return high, (x - high.astype(f32)).astype(bf16)


def thirds(x):
    high = x.astype(bf16).astype(f32)
    rest = x - high
    mid = rest.astype(bf16).astype(f32)
    return high, mid, rest - mid


def split_dot(a, b, dims=KM):
    return mm(a[0], b[0], dims) + (mm(a[0], b[1], dims) + mm(a[1], b[0], dims))


def block_inverse(a):
    lane = lax.broadcasted_iota(jnp.int32, (WIDTH, NB), 1)
    row = lax.broadcasted_iota(jnp.int32, (WIDTH, NB), 0)
    lane_all = lax.broadcasted_iota(jnp.int32, (NB, NB), 1)
    for start in range(0, NB, WIDTH):
        stop = start + WIDTH
        p = a[start:stop, :]
        inside = (lane >= start) & (lane < stop)
        left = jnp.where(inside, 0.0, jnp.where(lane < start, -p, p))
        h, m, l = thirds(left)
        lhs = jnp.concatenate([h, h, m, h, l, m], axis=0).T.astype(bf16)
        cols = [jnp.broadcast_to(p[:, start + j : start + j + 1], (WIDTH, NB)) for j in range(WIDTH)]
        x = jnp.where(inside, jnp.where(lane - start == row, 1.0, 0.0), p)
        for j in range(WIDTH):
            c = cols[j]
            scale = 1.0 / c[j : j + 1, :]
            here = row == j

            def step(v):
                t = v[j : j + 1, :] * scale
                return jnp.where(here, t, v - c * t)

            for i in range(j + 1, WIDTH):
                cols[i] = step(cols[i])
            x = step(x)
        h, m, l = thirds(x)
        rhs = jnp.concatenate([h, m, h, l, h, m], axis=0).astype(bf16)
        a = jnp.where((lane_all >= start) & (lane_all < stop), 0.0, a) - mm(lhs, rhs)
        rows = [x]
        if start:
            rows = [a[:start]] + rows
        if stop < NB:
            rows = rows + [a[stop:]]
        a = jnp.concatenate(rows, axis=0)
    return a


def inverse_kernel(with_rows, sid_ref, g_ref, x_ref, *rest):
    size = x_ref.shape[0]
    count = size // NB
    for k in range(count):
        s, n = slice(k * NB, (k + 1) * NB), (k + 1) % count
        t = slice(n * NB, (n + 1) * NB)
        x_ref[s, s] = g_ref[k, :NB, :]
        block = g_ref[k, NB : 2 * NB, :]
        x_ref[s, t] = block
        x_ref[t, s] = block.T
    for p in range(2):
        s, t = slice(p * NB, (p + 1) * NB), slice((p + 2) * NB, (p + 3) * NB)
        block = jnp.concatenate([g_ref[p, 2 * NB :, :], g_ref[p + 2, 2 * NB :, :]], axis=0)
        x_ref[s, t] = block
        x_ref[t, s] = block.T
    if with_rows:
        rest[0][...] = x_ref[pl.ds(pl.multiple_of(sid_ref[0] * NB, NB), NB), :]
    for b in range(count):
        s = slice(b * NB, (b + 1) * NB)
        inv = block_inverse(x_ref[s, s])
        rows = x_ref[s, :]
        lane = lax.broadcasted_iota(jnp.int32, (NB, size), 1)
        inside = (lane >= b * NB) & (lane < (b + 1) * NB)
        left = jnp.where(lane < b * NB, -rows, rows)
        w = split_dot(halves(inv), halves(jnp.where(inside, 0.0, rows)))
        w = jnp.concatenate([inv if c == b else w[:, c * NB : (c + 1) * NB] for c in range(count)], axis=1)
        w_halves = halves(w)
        for o in [*range(b + 1, count), *range(b)]:
            os = slice(o * NB, (o + 1) * NB)
            kept = [jnp.zeros((NB, NB), f32) if c == b else x_ref[os, c * NB : (c + 1) * NB] for c in range(count)]
            x_ref[os, :] = jnp.concatenate(kept, axis=1) - split_dot(halves(left[:, os].T), w_halves)
        x_ref[s, :] = w


def inverse(sid, g, with_rows=False):
    size = 4 * NB
    outs = [jax.ShapeDtypeStruct((size, size), f32)]
    if with_rows:
        outs.append(jax.ShapeDtypeStruct((NB, size), f32))
    return pl.pallas_call(
        functools.partial(inverse_kernel, with_rows),
        out_shape=outs,
        in_specs=[SMEM, VMEM],
        out_specs=[VMEM] * len(outs),
        compiler_params=PARAMS,
        cost_estimate=pl.CostEstimate(flops=60 * size**3, bytes_accessed=8 * size * size, transcendentals=0),
        name="inverse",
    )(sid, g)


def weigh_kernel(total_slots, ids_ref, design_ref, process_ref, own_ref, ahead_ref):
    rows = own_ref.shape[0] // 2
    me, live_count = ids_ref[0], ids_ref[1]
    own_seen = jnp.int32(0)
    for r in range(4):
        target = ids_ref[2 + r]
        is_own = target == me
        live = (r < live_count) & (is_own | (target == me + 1))
        h = design_ref[r * rows : (r + 1) * rows, :].astype(f32)
        mean_sq = jnp.mean(h * h, axis=-1, keepdims=True)
        w = h * lax.rsqrt(4.0 * total_slots * (mean_sq + 1e-06))
        w = jnp.where(live, w, 0.0).astype(bf16)
        ahead_seen = r - own_seen

        @pl.when(is_own)
        def _():
            own_ref[pl.ds(jnp.minimum(own_seen, 1) * rows, rows), :] = w

        @pl.when(jnp.logical_not(is_own))
        def _():
            ahead_ref[pl.ds(jnp.minimum(ahead_seen, 1) * rows, rows), :] = w

        own_seen = own_seen + jnp.where(is_own, 1, 0)
    ahead_ref[2 * rows :, :] = process_ref[...]


def gram_kernel(own_ref, incoming_ref, out_ref):
    both = jnp.concatenate([own_ref[...], incoming_ref[: own_ref.shape[0], :]], axis=0)
    g = mm(both, both, KK)
    for k in range(4):
        n, p, h = (k + 1) % 4, k % 2, HALF * (k // 2)
        out_ref[k, :NB, :] = g[k * NB : (k + 1) * NB, k * NB : (k + 1) * NB]
        out_ref[k, NB : 2 * NB, :] = g[k * NB : (k + 1) * NB, n * NB : (n + 1) * NB]
        out_ref[k, 2 * NB :, :] = g[p * NB + h : p * NB + h + HALF, (p + 2) * NB : (p + 3) * NB]


def start_kernel(sid_ref, parts_ref, own_ref, incoming_ref, prior_ref, d_ref, copies_ref):
    q = sid_ref[0]
    rows = own_ref[...].astype(f32) + incoming_ref[incoming_ref.shape[0] - NB :, :].astype(f32)
    total = (parts_ref[0] + parts_ref[1]) + (parts_ref[2] + parts_ref[3])

    def block(k):
        out = rows[:, :NB]
        for j in range(1, 4):
            out = jnp.where(k == j, rows[:, j * NB : (j + 1) * NB], out)
        return out

    unit = lax.broadcasted_iota(jnp.int32, (NB, NB), 0) == lax.broadcasted_iota(jnp.int32, (NB, NB), 1)
    across = block(lax.rem(q + 2, 4))
    half = jnp.where(q < 2, across[:HALF, :], across.T[HALF:, :])
    d = jnp.concatenate(
        [
            total[:NB] + (block(q) + jnp.where(unit, prior_ref[...], 0.0)),
            total[NB : 2 * NB] + block(lax.rem(q + 1, 4)),
            total[2 * NB :] + half,
        ],
        axis=0,
    )
    d_ref[...] = d
    for k in range(4):
        copies_ref[k] = d


def next_kernel(d_in, left_ref, right_ref, d_ref, copies_ref):
    d = d_in[...] - left_ref[...] - right_ref[...]
    d_ref[...] = d
    for k in range(4):
        copies_ref[k] = d


def sliced_terms_kernel(sid_ref, x_ref, a_ref, c_ref, right_term, left_term, lhs, flipped):
    q = sid_ref[0]
    p, h = lax.rem(q, 2), pl.multiple_of(lax.div(q, 2) * HALF, HALF)

    def at(k):
        return pl.ds(pl.multiple_of(k * NB, NB), NB)

    own, after, across = at(q), at(lax.rem(q + 1, 4)), at(p + 2)
    lhs[:NB, :] = a_ref[own, :].astype(f32)
    lhs[NB : NB + HALF, :] = a_ref[pl.ds(pl.multiple_of(p * NB + h, HALF), HALF), :].astype(f32)
    lhs[NB + HALF : 2 * NB + HALF, :] = c_ref[:, own].astype(f32).T
    flipped[...] = c_ref[:, at(p)].astype(f32).T
    lhs[2 * NB + HALF :, :] = flipped[pl.ds(h, HALF), :]
    z = halves(split_dot(halves(lhs[...]), halves(x_ref[...])))

    def rows(first, count):
        return z[0][first : first + count], z[1][first : first + count]

    full, part = rows(0, NB), rows(NB, HALF)
    right_term[:NB, :] = cross_dot(full, a_ref[own, :], MK)
    right_term[NB : 2 * NB, :] = cross_dot(full, a_ref[after, :], MK)
    right_term[2 * NB :, :] = cross_dot(part, a_ref[across, :], MK)
    full, part = rows(NB + HALF, NB), rows(2 * NB + HALF, HALF)
    left_term[:NB, :] = cross_dot(full, c_ref[:, own])
    left_term[NB : 2 * NB, :] = cross_dot(full, c_ref[:, after])
    left_term[2 * NB :, :] = cross_dot(part, c_ref[:, across])


def sliced_terms(sid, x, a, c):
    size = x.shape[0]
    out = jax.ShapeDtypeStruct((2 * NB + HALF, NB), f32)
    return pl.pallas_call(
        sliced_terms_kernel,
        out_shape=(out, out),
        in_specs=[SMEM] + [VMEM] * 3,
        out_specs=(VMEM, VMEM),
        scratch_shapes=[pltpu.VMEM((3 * NB, size), f32), pltpu.VMEM((NB, size), f32)],
        compiler_params=PARAMS,
        cost_estimate=pl.CostEstimate(flops=4 * size**3, bytes_accessed=16 * size * size, transcendentals=0),
        name="sliced_terms",
    )(sid, x, a, c)


def terms_kernel(sid_ref, x_ref, a_ref, c_ref, *outs):
    col = pl.multiple_of(sid_ref[0] * NB, NB)
    lhs = jnp.concatenate([a_ref[pl.ds(col, NB), :].astype(f32), c_ref[:, pl.ds(col, NB)].astype(f32).T], axis=0)
    z = halves(split_dot(halves(lhs), halves(x_ref[...])))
    top = z[0][:NB], z[1][:NB]
    outs[0][...] = cross_dot(top, a_ref[...], MK)
    both = cross_dot(z, c_ref[...])
    outs[1][...] = both[NB:]
    outs[2][...] = -both[:NB]


def cross_dot(a, b, dims=KM):
    if b.dtype == bf16:
        return mm(a[0], b, dims) + mm(a[1], b, dims)
    return split_dot(a, halves(b), dims)


def terms(sid, x, a, c):
    size = x.shape[0]
    out = jax.ShapeDtypeStruct((NB, size), f32)
    return pl.pallas_call(
        terms_kernel,
        out_shape=(out,) * 3,
        in_specs=[SMEM] + [VMEM] * 3,
        out_specs=(VMEM,) * 3,
        compiler_params=PARAMS,
        cost_estimate=pl.CostEstimate(flops=4 * size**3, bytes_accessed=16 * size * size, transcendentals=0),
        name="terms",
    )(sid, x, a, c)


def coupling_kernel(x_ref, a_ref, c_ref, n_ref):
    x = halves(x_ref[...])
    if a_ref.dtype == bf16:
        z = mm(a_ref[...], x[0]) + mm(a_ref[...], x[1])
    else:
        z = split_dot(halves(a_ref[...]), x)
    n_ref[...] = -cross_dot(halves(z), c_ref[...])


def coupled(x, a, c):
    size = x.shape[0]
    return pl.pallas_call(
        coupling_kernel,
        out_shape=jax.ShapeDtypeStruct(x.shape, f32),
        in_specs=[VMEM] * 3,
        out_specs=VMEM,
        compiler_params=PARAMS,
        cost_estimate=pl.CostEstimate(flops=12 * size**3, bytes_accessed=16 * size * size, transcendentals=0),
        name="coupling",
    )(x, a, c)


def passed_along(block, axis, distance, around=False):
    count = lax.axis_size(axis)
    route = [(i, (i + distance) % count) for i in range(count) if around or 0 <= i + distance < count]
    return lax.ppermute(block, axis, route)


def exchanged(blocks):
    return lax.all_to_all(blocks, "swath", 0, 0, tiled=True)


def shards(design, process, prior_prec, routes, counts):
    row_count, size = process.shape[1:]
    swaths = lax.axis_size("swath")
    me = lax.axis_index("tm")
    sid = lax.axis_index("swath")
    total_slots = design.shape[1] * swaths
    ids = jnp.concatenate([me[None].astype(jnp.int32), counts[0], routes[0]])
    sids = sid[None].astype(jnp.int32)
    half = design.shape[1] // 2
    own, ahead = pl.pallas_call(
        functools.partial(weigh_kernel, total_slots),
        out_shape=(
            jax.ShapeDtypeStruct((half, size), bf16),
            jax.ShapeDtypeStruct((half + row_count, size), bf16),
        ),
        in_specs=[SMEM] + [VMEM] * 2,
        out_specs=(VMEM, VMEM),
        compiler_params=PARAMS,
        name="weigh",
    )(ids, design[0], process[0])
    incoming = passed_along(ahead, "tm", 1)
    cut = jax.ShapeDtypeStruct((2 * NB + HALF, NB), f32)
    cuts = jax.ShapeDtypeStruct((swaths,) + cut.shape, f32)
    parts = pl.pallas_call(
        gram_kernel,
        out_shape=cuts,
        in_specs=[VMEM] * 2,
        out_specs=VMEM,
        compiler_params=PARAMS,
        name="gram",
    )(own, incoming)
    diag, copies = pl.pallas_call(
        start_kernel,
        out_shape=(cut, cuts),
        in_specs=[SMEM] + [VMEM] * 4,
        out_specs=(VMEM, VMEM),
        compiler_params=PARAMS,
        name="start",
    )(sids, exchanged(parts), process[0], incoming, prior_prec)
    pair = -jnp.concatenate([incoming[half:], process[0]], axis=0)
    copies, pair = lax.optimization_barrier((copies, pair))
    all_diag = exchanged(copies)
    pairs = exchanged(jnp.broadcast_to(pair[None], (swaths,) + pair.shape))
    (x,) = inverse(sids, all_diag)
    a = pairs[:, :row_count].reshape(size, size)
    c = pairs[:, row_count:].reshape(size, size)
    rows = None
    for level in range(LEVELS):
        distance = 2**level
        if level == LEVELS - 1:
            out = terms(sids, x, a, c)
            from_right = passed_along(out[0], "tm", -distance)
            from_left = passed_along(out[1], "tm", distance)
            coupling = passed_along(out[2], "tm", -distance)
            return ((rows - from_left - from_right)[None], coupling[None])
        right_term, left_term = sliced_terms(sids, x, a, c)
        from_right = passed_along(right_term, "tm", -distance)
        from_left = passed_along(left_term, "tm", distance)
        n = coupled(x, a, c)
        from_right, from_left, n = lax.optimization_barrier((from_right, from_left, n))
        diag, copies = pl.pallas_call(
            next_kernel,
            out_shape=(cut, cuts),
            in_specs=[VMEM] * 3,
            out_specs=(VMEM, VMEM),
            compiler_params=PARAMS,
            name="next",
        )(diag, from_left, from_right)
        x, *tail = inverse(sids, exchanged(copies), level == LEVELS - 2)
        rows = tail[0] if tail else None
        a = passed_along(n, "tm", distance)
        c = passed_along(n, "tm", -distance)


def solution(mesh):
    return jax.shard_map(
        shards,
        mesh=mesh,
        in_specs=(
            P("tm", "swath", None),
            P("tm", "swath", None),
            P("tm", "swath"),
            P("tm", "swath"),
            P("tm", "swath"),
        ),
        out_specs=(P("tm", "swath", None), P("tm", "swath", None)),
        check_vma=False,
    )
```

```python
import functools
import jax
import jax.numpy as jnp
from jax import lax
from jax.experimental import pallas as pl
from jax.experimental.pallas import tpu as pltpu
from jax.sharding import PartitionSpec as P

LEVELS = 3
NB = 128
WIDTH = 16
HALF = NB // 2
f32, bf16 = jnp.float32, jnp.bfloat16
VMEM = pl.BlockSpec(memory_space=pltpu.VMEM)
SMEM = pl.BlockSpec(memory_space=pltpu.SMEM)
PARAMS = pltpu.CompilerParams(vmem_limit_bytes=48 * 2**20)
KK, KM, MK = ((0,), (0,)), ((1,), (0,)), ((1,), (1,))


def mm(a, b, dims=KM):
    return lax.dot_general(a, b, (dims, ((), ())), preferred_element_type=f32)


def halves(x):
    high = x.astype(bf16)
    return high, (x - high.astype(f32)).astype(bf16)


def thirds(x):
    high = x.astype(bf16).astype(f32)
    rest = x - high
    mid = rest.astype(bf16).astype(f32)
    return high, mid, rest - mid


def split_dot(a, b, dims=KM):
    return mm(a[0], b[0], dims) + (mm(a[0], b[1], dims) + mm(a[1], b[0], dims))


def block_inverse(a):
    lane = lax.broadcasted_iota(jnp.int32, (WIDTH, NB), 1)
    row = lax.broadcasted_iota(jnp.int32, (WIDTH, NB), 0)
    lane_all = lax.broadcasted_iota(jnp.int32, (NB, NB), 1)
    p = a[:WIDTH, :]
    for start in range(0, NB, WIDTH):
        stop = start + WIDTH
        inside = (lane >= start) & (lane < stop)
        cols = [jnp.broadcast_to(p[:, start + j : start + j + 1], (WIDTH, NB)) for j in range(WIDTH)]
        h, m, l = thirds(jnp.where(inside, 0.0, jnp.where(lane < start, -p, p)))
        lhs = jnp.concatenate([h, h, m, h, l, m], axis=0).T.astype(bf16)
        x = jnp.where(inside, jnp.where(lane - start == row, 1.0, 0.0), p)
        if stop < NB:
            after = a[stop : stop + WIDTH, :]
            weights = [jnp.broadcast_to(after[:, start + j : start + j + 1], (WIDTH, NB)) for j in range(WIDTH)]
        for j in range(WIDTH):
            c = cols[j]
            scale = 1.0 / c[j : j + 1, :]
            here = row == j

            def step(v):
                t = v[j : j + 1, :] * scale
                return jnp.where(here, t, v - c * t)

            for i in range(j + 1, WIDTH):
                cols[i] = step(cols[i])
            x = step(x)
        if stop < NB:
            sums = [weights[j] * x[j : j + 1, :] for j in range(4)]
            for j in range(4, WIDTH):
                sums[j % 4] = sums[j % 4] + weights[j] * x[j : j + 1, :]
            p = jnp.where(inside, 0.0, after) - ((sums[0] + sums[1]) + (sums[2] + sums[3]))
        h, m, l = thirds(x)
        rhs = jnp.concatenate([h, m, h, l, h, m], axis=0).astype(bf16)
        a = jnp.where((lane_all >= start) & (lane_all < stop), 0.0, a) - mm(lhs, rhs)
        rows = [x]
        if start:
            rows = [a[:start]] + rows
        if stop < NB:
            rows = rows + [a[stop:]]
        a = jnp.concatenate(rows, axis=0)
    return a


def inverse_kernel(with_rows, sid_ref, g_ref, x_ref, *rest):
    size = x_ref.shape[0]
    count = size // NB
    for k in range(count):
        s, n = slice(k * NB, (k + 1) * NB), (k + 1) % count
        t = slice(n * NB, (n + 1) * NB)
        x_ref[s, s] = g_ref[k, :NB, :]
        block = g_ref[k, NB : 2 * NB, :]
        x_ref[s, t] = block
        x_ref[t, s] = block.T
    for p in range(2):
        s, t = slice(p * NB, (p + 1) * NB), slice((p + 2) * NB, (p + 3) * NB)
        block = jnp.concatenate([g_ref[p, 2 * NB :, :], g_ref[p + 2, 2 * NB :, :]], axis=0)
        x_ref[s, t] = block
        x_ref[t, s] = block.T
    if with_rows:
        rest[0][...] = x_ref[pl.ds(pl.multiple_of(sid_ref[0] * NB, NB), NB), :]
    for b in range(count):
        s = slice(b * NB, (b + 1) * NB)
        inv = block_inverse(x_ref[s, s])
        rows = x_ref[s, :]
        lane = lax.broadcasted_iota(jnp.int32, (NB, size), 1)
        inside = (lane >= b * NB) & (lane < (b + 1) * NB)
        left = jnp.where(lane < b * NB, -rows, rows)
        w = split_dot(halves(inv), halves(jnp.where(inside, 0.0, rows)))
        w = jnp.concatenate([inv if c == b else w[:, c * NB : (c + 1) * NB] for c in range(count)], axis=1)
        w_halves = halves(w)
        for o in [*range(b + 1, count), *range(b)]:
            os = slice(o * NB, (o + 1) * NB)
            kept = [jnp.zeros((NB, NB), f32) if c == b else x_ref[os, c * NB : (c + 1) * NB] for c in range(count)]
            x_ref[os, :] = jnp.concatenate(kept, axis=1) - split_dot(halves(left[:, os].T), w_halves)
        x_ref[s, :] = w


def inverse(sid, g, with_rows=False):
    size = 4 * NB
    outs = [jax.ShapeDtypeStruct((size, size), f32)]
    if with_rows:
        outs.append(jax.ShapeDtypeStruct((NB, size), f32))
    return pl.pallas_call(
        functools.partial(inverse_kernel, with_rows),
        out_shape=outs,
        in_specs=[SMEM, VMEM],
        out_specs=[VMEM] * len(outs),
        compiler_params=PARAMS,
        cost_estimate=pl.CostEstimate(flops=60 * size**3, bytes_accessed=8 * size * size, transcendentals=0),
        name="inverse",
    )(sid, g)


def weigh_kernel(total_slots, ids_ref, design_ref, process_ref, own_ref, ahead_ref, copies_ref):
    rows = own_ref.shape[0] // 2
    me, live_count = ids_ref[0], ids_ref[1]
    own_seen = jnp.int32(0)
    for r in range(4):
        target = ids_ref[2 + r]
        is_own = target == me
        live = (r < live_count) & (is_own | (target == me + 1))
        h = design_ref[r * rows : (r + 1) * rows, :].astype(f32)
        mean_sq = jnp.mean(h * h, axis=-1, keepdims=True)
        w = h * lax.rsqrt(4.0 * total_slots * (mean_sq + 1e-06))
        w = jnp.where(live, w, 0.0).astype(bf16)
        ahead_seen = r - own_seen

        @pl.when(is_own)
        def _():
            own_ref[pl.ds(jnp.minimum(own_seen, 1) * rows, rows), :] = w

        @pl.when(jnp.logical_not(is_own))
        def _():
            ahead_ref[pl.ds(jnp.minimum(ahead_seen, 1) * rows, rows), :] = w

        own_seen = own_seen + jnp.where(is_own, 1, 0)
    ahead_ref[2 * rows :, :] = process_ref[...]
    for k in range(4):
        copies_ref[k] = process_ref[...]


def gram_kernel(own_ref, incoming_ref, out_ref):
    both = jnp.concatenate([own_ref[...], incoming_ref[: own_ref.shape[0], :]], axis=0)
    g = mm(both, both, KK)
    for k in range(4):
        n, p, h = (k + 1) % 4, k % 2, HALF * (k // 2)
        out_ref[k, :NB, :] = g[k * NB : (k + 1) * NB, k * NB : (k + 1) * NB]
        out_ref[k, NB : 2 * NB, :] = g[k * NB : (k + 1) * NB, n * NB : (n + 1) * NB]
        out_ref[k, 2 * NB :, :] = g[p * NB + h : p * NB + h + HALF, (p + 2) * NB : (p + 3) * NB]


def start_kernel(sid_ref, parts_ref, own_ref, incoming_ref, prior_ref, d_ref, copies_ref):
    q = sid_ref[0]
    rows = own_ref[...].astype(f32) + incoming_ref[incoming_ref.shape[0] - NB :, :].astype(f32)
    total = (parts_ref[0] + parts_ref[1]) + (parts_ref[2] + parts_ref[3])

    def block(k):
        out = rows[:, :NB]
        for j in range(1, 4):
            out = jnp.where(k == j, rows[:, j * NB : (j + 1) * NB], out)
        return out

    unit = lax.broadcasted_iota(jnp.int32, (NB, NB), 0) == lax.broadcasted_iota(jnp.int32, (NB, NB), 1)
    across = block(lax.rem(q + 2, 4))
    half = jnp.where(q < 2, across[:HALF, :], across.T[HALF:, :])
    d = jnp.concatenate(
        [
            total[:NB] + (block(q) + jnp.where(unit, prior_ref[...], 0.0)),
            total[NB : 2 * NB] + block(lax.rem(q + 1, 4)),
            total[2 * NB :] + half,
        ],
        axis=0,
    )
    d_ref[...] = d
    for k in range(4):
        copies_ref[k] = d


def next_kernel(d_in, left_ref, right_ref, d_ref, copies_ref):
    d = d_in[...] - left_ref[...] - right_ref[...]
    d_ref[...] = d
    for k in range(4):
        copies_ref[k] = d


def sliced_terms_kernel(sid_ref, x_ref, a_ref, c_ref, right_term, left_term, lhs, flipped):
    q = sid_ref[0]
    p, h = lax.rem(q, 2), pl.multiple_of(lax.div(q, 2) * HALF, HALF)

    def at(k):
        return pl.ds(pl.multiple_of(k * NB, NB), NB)

    own, after, across = at(q), at(lax.rem(q + 1, 4)), at(p + 2)
    lhs[:NB, :] = a_ref[own, :].astype(f32)
    lhs[NB : NB + HALF, :] = a_ref[pl.ds(pl.multiple_of(p * NB + h, HALF), HALF), :].astype(f32)
    lhs[NB + HALF : 2 * NB + HALF, :] = c_ref[:, own].astype(f32).T
    flipped[...] = c_ref[:, at(p)].astype(f32).T
    lhs[2 * NB + HALF :, :] = flipped[pl.ds(h, HALF), :]
    z = halves(split_dot(halves(lhs[...]), halves(x_ref[...])))

    def rows(first, count):
        return z[0][first : first + count], z[1][first : first + count]

    full, part = rows(0, NB), rows(NB, HALF)
    right_term[:NB, :] = cross_dot(full, a_ref[own, :], MK)
    right_term[NB : 2 * NB, :] = cross_dot(full, a_ref[after, :], MK)
    right_term[2 * NB :, :] = cross_dot(part, a_ref[across, :], MK)
    full, part = rows(NB + HALF, NB), rows(2 * NB + HALF, HALF)
    left_term[:NB, :] = cross_dot(full, c_ref[:, own])
    left_term[NB : 2 * NB, :] = cross_dot(full, c_ref[:, after])
    left_term[2 * NB :, :] = cross_dot(part, c_ref[:, across])


def sliced_terms(sid, x, a, c):
    size = x.shape[0]
    out = jax.ShapeDtypeStruct((2 * NB + HALF, NB), f32)
    return pl.pallas_call(
        sliced_terms_kernel,
        out_shape=(out, out),
        in_specs=[SMEM] + [VMEM] * 3,
        out_specs=(VMEM, VMEM),
        scratch_shapes=[pltpu.VMEM((3 * NB, size), f32), pltpu.VMEM((NB, size), f32)],
        compiler_params=PARAMS,
        cost_estimate=pl.CostEstimate(flops=4 * size**3, bytes_accessed=16 * size * size, transcendentals=0),
        name="sliced_terms",
    )(sid, x, a, c)


def terms_kernel(sid_ref, x_ref, a_ref, c_ref, *outs):
    col = pl.multiple_of(sid_ref[0] * NB, NB)
    lhs = jnp.concatenate([a_ref[pl.ds(col, NB), :].astype(f32), c_ref[:, pl.ds(col, NB)].astype(f32).T], axis=0)
    z = halves(split_dot(halves(lhs), halves(x_ref[...])))
    top = z[0][:NB], z[1][:NB]
    outs[0][...] = cross_dot(top, a_ref[...], MK).astype(bf16)
    both = cross_dot(z, c_ref[...])
    outs[1][...] = both[NB:].astype(bf16)
    outs[2][...] = -both[:NB]


def cross_dot(a, b, dims=KM):
    if b.dtype == bf16:
        return mm(a[0], b, dims) + mm(a[1], b, dims)
    return split_dot(a, halves(b), dims)


def terms(sid, x, a, c):
    size = x.shape[0]
    term = jax.ShapeDtypeStruct((NB, size), bf16)
    return pl.pallas_call(
        terms_kernel,
        out_shape=(term, term, jax.ShapeDtypeStruct((NB, size), f32)),
        in_specs=[SMEM] + [VMEM] * 3,
        out_specs=(VMEM,) * 3,
        compiler_params=PARAMS,
        cost_estimate=pl.CostEstimate(flops=4 * size**3, bytes_accessed=16 * size * size, transcendentals=0),
        name="terms",
    )(sid, x, a, c)


def coupling_kernel(x_ref, a_ref, c_ref, n_ref):
    x = halves(x_ref[...])
    if a_ref.dtype == bf16:
        z = mm(a_ref[...], x[0]) + mm(a_ref[...], x[1])
    else:
        z = split_dot(halves(a_ref[...]), x)
    n_ref[...] = -cross_dot(halves(z), c_ref[...])


def coupled(x, a, c):
    size = x.shape[0]
    return pl.pallas_call(
        coupling_kernel,
        out_shape=jax.ShapeDtypeStruct(x.shape, f32),
        in_specs=[VMEM] * 3,
        out_specs=VMEM,
        compiler_params=PARAMS,
        cost_estimate=pl.CostEstimate(flops=12 * size**3, bytes_accessed=16 * size * size, transcendentals=0),
        name="coupling",
    )(x, a, c)


def passed_along(block, axis, distance, around=False):
    count = lax.axis_size(axis)
    route = [(i, (i + distance) % count) for i in range(count) if around or 0 <= i + distance < count]
    return lax.ppermute(block, axis, route)


def exchanged(blocks):
    return lax.all_to_all(blocks, "swath", 0, 0, tiled=True)


def shards(design, process, prior_prec, routes, counts):
    row_count, size = process.shape[1:]
    swaths = lax.axis_size("swath")
    me = lax.axis_index("tm")
    sid = lax.axis_index("swath")
    total_slots = design.shape[1] * swaths
    ids = jnp.concatenate([me[None].astype(jnp.int32), counts[0], routes[0]])
    sids = sid[None].astype(jnp.int32)
    half = design.shape[1] // 2
    own, ahead, process_copies = pl.pallas_call(
        functools.partial(weigh_kernel, total_slots),
        out_shape=(
            jax.ShapeDtypeStruct((half, size), bf16),
            jax.ShapeDtypeStruct((half + row_count, size), bf16),
            jax.ShapeDtypeStruct((swaths, row_count, size), bf16),
        ),
        in_specs=[SMEM] + [VMEM] * 2,
        out_specs=(VMEM, VMEM, VMEM),
        compiler_params=PARAMS,
        name="weigh",
    )(ids, design[0], process[0])
    incoming = passed_along(ahead, "tm", 1)
    cut = jax.ShapeDtypeStruct((2 * NB + HALF, NB), f32)
    cuts = jax.ShapeDtypeStruct((swaths,) + cut.shape, f32)
    parts = pl.pallas_call(
        gram_kernel,
        out_shape=cuts,
        in_specs=[VMEM] * 2,
        out_specs=VMEM,
        compiler_params=PARAMS,
        name="gram",
    )(own, incoming)
    parts, c = lax.optimization_barrier((parts, exchanged(process_copies)))
    c = c.reshape(size, size)
    diag, copies = pl.pallas_call(
        start_kernel,
        out_shape=(cut, cuts),
        in_specs=[SMEM] + [VMEM] * 4,
        out_specs=(VMEM, VMEM),
        compiler_params=PARAMS,
        name="start",
    )(sids, exchanged(parts), process[0], incoming, prior_prec)
    a = passed_along(c, "tm", 1)
    (x,) = inverse(sids, exchanged(copies))
    rows = None
    for level in range(LEVELS):
        distance = 2**level
        if level == LEVELS - 1:
            out = terms(sids, x, a, c)
            from_right = passed_along(out[0], "tm", -distance)
            from_left = passed_along(out[1], "tm", distance)
            coupling = passed_along(out[2], "tm", -distance)
            return ((rows - from_left.astype(f32) - from_right.astype(f32))[None], coupling[None])
        right_term, left_term = sliced_terms(sids, x, a, c)
        from_right = passed_along(right_term, "tm", -distance)
        from_left = passed_along(left_term, "tm", distance)
        n = coupled(x, a, c)
        from_right, from_left, n = lax.optimization_barrier((from_right, from_left, n))
        diag, copies = pl.pallas_call(
            next_kernel,
            out_shape=(cut, cuts),
            in_specs=[VMEM] * 3,
            out_specs=(VMEM, VMEM),
            compiler_params=PARAMS,
            name="next",
        )(diag, from_left, from_right)
        x, *tail = inverse(sids, exchanged(copies), level == LEVELS - 2)
        rows = tail[0] if tail else None
        a = passed_along(n, "tm", distance)
        c = passed_along(n, "tm", -distance)


def solution(mesh):
    return jax.shard_map(
        shards,
        mesh=mesh,
        in_specs=(
            P("tm", "swath", None),
            P("tm", "swath", None),
            P("tm", "swath"),
            P("tm", "swath"),
            P("tm", "swath"),
        ),
        out_specs=(P("tm", "swath", None), P("tm", "swath", None)),
        check_vma=False,
    )
```

```python
import functools
import jax
import jax.numpy as jnp
from jax import lax
from jax.experimental import pallas as pl
from jax.experimental.pallas import tpu as pltpu
from jax.sharding import PartitionSpec as P

LEVELS = 3
NB = 128
WIDTH = 16
HALF = NB // 2
f32, bf16 = jnp.float32, jnp.bfloat16
VMEM = pl.BlockSpec(memory_space=pltpu.VMEM)
SMEM = pl.BlockSpec(memory_space=pltpu.SMEM)
PARAMS = pltpu.CompilerParams(vmem_limit_bytes=48 * 2**20)
KK, KM, MK = ((0,), (0,)), ((1,), (0,)), ((1,), (1,))


def mm(a, b, dims=KM):
    return lax.dot_general(a, b, (dims, ((), ())), preferred_element_type=f32)


def halves(x):
    high = x.astype(bf16)
    return high, (x - high.astype(f32)).astype(bf16)


def thirds(x):
    high = x.astype(bf16).astype(f32)
    rest = x - high
    mid = rest.astype(bf16).astype(f32)
    return high, mid, rest - mid


def split_dot(a, b, dims=KM):
    return mm(a[0], b[0], dims) + (mm(a[0], b[1], dims) + mm(a[1], b[0], dims))


def block_inverse(a):
    lane = lax.broadcasted_iota(jnp.int32, (WIDTH, NB), 1)
    row = lax.broadcasted_iota(jnp.int32, (WIDTH, NB), 0)
    lane_all = lax.broadcasted_iota(jnp.int32, (NB, NB), 1)
    p = a[:WIDTH, :]
    for start in range(0, NB, WIDTH):
        stop = start + WIDTH
        inside = (lane >= start) & (lane < stop)
        cols = [jnp.broadcast_to(p[:, start + j : start + j + 1], (WIDTH, NB)) for j in range(WIDTH)]
        h, m, l = thirds(jnp.where(inside, 0.0, jnp.where(lane < start, -p, p)))
        lhs = jnp.concatenate([h, h, m, h, l, m], axis=0).T.astype(bf16)
        x = jnp.where(inside, jnp.where(lane - start == row, 1.0, 0.0), p)
        if stop < NB:
            after = a[stop : stop + WIDTH, :]
            weights = [jnp.broadcast_to(after[:, start + j : start + j + 1], (WIDTH, NB)) for j in range(WIDTH)]
        for j in range(WIDTH):
            c = cols[j]
            scale = 1.0 / c[j : j + 1, :]
            here = row == j

            def step(v):
                t = v[j : j + 1, :] * scale
                return jnp.where(here, t, v - c * t)

            for i in range(j + 1, WIDTH):
                cols[i] = step(cols[i])
            x = step(x)
        if stop < NB:
            sums = [weights[j] * x[j : j + 1, :] for j in range(4)]
            for j in range(4, WIDTH):
                sums[j % 4] = sums[j % 4] + weights[j] * x[j : j + 1, :]
            p = jnp.where(inside, 0.0, after) - ((sums[0] + sums[1]) + (sums[2] + sums[3]))
        h, m, l = thirds(x)
        rhs = jnp.concatenate([h, m, h, l, h, m], axis=0).astype(bf16)
        a = jnp.where((lane_all >= start) & (lane_all < stop), 0.0, a) - mm(lhs, rhs)
        rows = [x]
        if start:
            rows = [a[:start]] + rows
        if stop < NB:
            rows = rows + [a[stop:]]
        a = jnp.concatenate(rows, axis=0)
    return a


def inverse_kernel(with_rows, sid_ref, g_ref, x_ref, *rest):
    size = x_ref.shape[0]
    count = size // NB
    for k in range(count):
        s, n = slice(k * NB, (k + 1) * NB), (k + 1) % count
        t = slice(n * NB, (n + 1) * NB)
        x_ref[s, s] = g_ref[k, :NB, :]
        block = g_ref[k, NB : 2 * NB, :]
        x_ref[s, t] = block
        x_ref[t, s] = block.T
    for p in range(2):
        s, t = slice(p * NB, (p + 1) * NB), slice((p + 2) * NB, (p + 3) * NB)
        block = jnp.concatenate([g_ref[p, 2 * NB :, :], g_ref[p + 2, 2 * NB :, :]], axis=0)
        x_ref[s, t] = block
        x_ref[t, s] = block.T
    if with_rows:
        rest[0][...] = x_ref[pl.ds(pl.multiple_of(sid_ref[0] * NB, NB), NB), :]
    left_t = rest[-1]
    lane = lax.broadcasted_iota(jnp.int32, (NB, size), 1)

    def eliminate(b, carry):
        first = pl.multiple_of(b * NB, NB)
        at = pl.ds(first, NB)
        inv = block_inverse(x_ref[at, at])
        rows = x_ref[at, :]
        inside = (lane >= first) & (lane < first + NB)
        left_t[...] = jnp.where(lane < first, -rows, rows).T
        w = split_dot(halves(inv), halves(jnp.where(inside, 0.0, rows)))
        w = jnp.where(inside, jnp.concatenate([inv] * count, axis=1), w)
        w_halves = halves(w)
        for i in range(1, count):
            other = pl.ds(pl.multiple_of(lax.rem(b + i, count) * NB, NB), NB)
            x_ref[other, :] = jnp.where(inside, 0.0, x_ref[other, :]) - split_dot(halves(left_t[other, :]), w_halves)
        x_ref[at, :] = w
        return carry

    lax.fori_loop(0, count, eliminate, 0)


def inverse(sid, g, with_rows=False):
    size = 4 * NB
    outs = [jax.ShapeDtypeStruct((size, size), f32)]
    if with_rows:
        outs.append(jax.ShapeDtypeStruct((NB, size), f32))
    return pl.pallas_call(
        functools.partial(inverse_kernel, with_rows),
        out_shape=outs,
        in_specs=[SMEM, VMEM],
        out_specs=[VMEM] * len(outs),
        scratch_shapes=[pltpu.VMEM((size, NB), f32)],
        compiler_params=PARAMS,
        cost_estimate=pl.CostEstimate(flops=60 * size**3, bytes_accessed=8 * size * size, transcendentals=0),
        name="inverse",
    )(sid, g)


def weigh_kernel(total_slots, ids_ref, design_ref, process_ref, own_ref, ahead_ref):
    rows = own_ref.shape[0] // 2
    me, live_count = ids_ref[0], ids_ref[1]
    own_seen = jnp.int32(0)
    for r in range(4):
        target = ids_ref[2 + r]
        is_own = target == me
        live = (r < live_count) & (is_own | (target == me + 1))
        h = design_ref[r * rows : (r + 1) * rows, :].astype(f32)
        mean_sq = jnp.mean(h * h, axis=-1, keepdims=True)
        w = h * lax.rsqrt(4.0 * total_slots * (mean_sq + 1e-06))
        w = jnp.where(live, w, 0.0).astype(bf16)
        ahead_seen = r - own_seen

        @pl.when(is_own)
        def _():
            own_ref[pl.ds(jnp.minimum(own_seen, 1) * rows, rows), :] = w

        @pl.when(jnp.logical_not(is_own))
        def _():
            ahead_ref[pl.ds(jnp.minimum(ahead_seen, 1) * rows, rows), :] = w

        own_seen = own_seen + jnp.where(is_own, 1, 0)
    ahead_ref[2 * rows :, :] = process_ref[...]


def gram_kernel(own_ref, incoming_ref, out_ref):
    both = jnp.concatenate([own_ref[...], incoming_ref[: own_ref.shape[0], :]], axis=0)
    g = mm(both, both, KK)
    for k in range(4):
        n, p, h = (k + 1) % 4, k % 2, HALF * (k // 2)
        out_ref[k, :NB, :] = g[k * NB : (k + 1) * NB, k * NB : (k + 1) * NB]
        out_ref[k, NB : 2 * NB, :] = g[k * NB : (k + 1) * NB, n * NB : (n + 1) * NB]
        out_ref[k, 2 * NB :, :] = g[p * NB + h : p * NB + h + HALF, (p + 2) * NB : (p + 3) * NB]


def start_kernel(sid_ref, parts_ref, own_ref, incoming_ref, prior_ref, d_ref, copies_ref):
    q = sid_ref[0]
    rows = own_ref[...].astype(f32) + incoming_ref[incoming_ref.shape[0] - NB :, :].astype(f32)
    total = (parts_ref[0] + parts_ref[1]) + (parts_ref[2] + parts_ref[3])

    def block(k):
        out = rows[:, :NB]
        for j in range(1, 4):
            out = jnp.where(k == j, rows[:, j * NB : (j + 1) * NB], out)
        return out

    unit = lax.broadcasted_iota(jnp.int32, (NB, NB), 0) == lax.broadcasted_iota(jnp.int32, (NB, NB), 1)
    across = block(lax.rem(q + 2, 4))
    half = jnp.where(q < 2, across[:HALF, :], across.T[HALF:, :])
    d = jnp.concatenate(
        [
            total[:NB] + (block(q) + jnp.where(unit, prior_ref[...], 0.0)),
            total[NB : 2 * NB] + block(lax.rem(q + 1, 4)),
            total[2 * NB :] + half,
        ],
        axis=0,
    )
    d_ref[...] = d
    for k in range(4):
        copies_ref[k] = d


def next_kernel(d_in, left_ref, right_ref, d_ref, copies_ref):
    d = d_in[...] - left_ref[...] - right_ref[...]
    d_ref[...] = d
    for k in range(4):
        copies_ref[k] = d


def sliced_terms_kernel(sid_ref, x_ref, a_ref, c_ref, right_term, left_term, lhs, flipped):
    q = sid_ref[0]
    p, h = lax.rem(q, 2), pl.multiple_of(lax.div(q, 2) * HALF, HALF)

    def at(k):
        return pl.ds(pl.multiple_of(k * NB, NB), NB)

    own, after, across = at(q), at(lax.rem(q + 1, 4)), at(p + 2)
    lhs[:NB, :] = a_ref[own, :].astype(f32)
    lhs[NB : NB + HALF, :] = a_ref[pl.ds(pl.multiple_of(p * NB + h, HALF), HALF), :].astype(f32)
    lhs[NB + HALF : 2 * NB + HALF, :] = c_ref[:, own].astype(f32).T
    flipped[...] = c_ref[:, at(p)].astype(f32).T
    lhs[2 * NB + HALF :, :] = flipped[pl.ds(h, HALF), :]
    z = halves(split_dot(halves(lhs[...]), halves(x_ref[...])))

    def rows(first, count):
        return z[0][first : first + count], z[1][first : first + count]

    full, part = rows(0, NB), rows(NB, HALF)
    right_term[:NB, :] = cross_dot(full, a_ref[own, :], MK)
    right_term[NB : 2 * NB, :] = cross_dot(full, a_ref[after, :], MK)
    right_term[2 * NB :, :] = cross_dot(part, a_ref[across, :], MK)
    full, part = rows(NB + HALF, NB), rows(2 * NB + HALF, HALF)
    left_term[:NB, :] = cross_dot(full, c_ref[:, own])
    left_term[NB : 2 * NB, :] = cross_dot(full, c_ref[:, after])
    left_term[2 * NB :, :] = cross_dot(part, c_ref[:, across])


def sliced_terms(sid, x, a, c):
    size = x.shape[0]
    out = jax.ShapeDtypeStruct((2 * NB + HALF, NB), f32)
    return pl.pallas_call(
        sliced_terms_kernel,
        out_shape=(out, out),
        in_specs=[SMEM] + [VMEM] * 3,
        out_specs=(VMEM, VMEM),
        scratch_shapes=[pltpu.VMEM((3 * NB, size), f32), pltpu.VMEM((NB, size), f32)],
        compiler_params=PARAMS,
        cost_estimate=pl.CostEstimate(flops=4 * size**3, bytes_accessed=16 * size * size, transcendentals=0),
        name="sliced_terms",
    )(sid, x, a, c)


def terms_kernel(sid_ref, x_ref, a_ref, c_ref, *outs):
    col = pl.multiple_of(sid_ref[0] * NB, NB)
    lhs = jnp.concatenate([a_ref[pl.ds(col, NB), :].astype(f32), c_ref[:, pl.ds(col, NB)].astype(f32).T], axis=0)
    z = halves(split_dot(halves(lhs), halves(x_ref[...])))
    top = z[0][:NB], z[1][:NB]
    outs[0][...] = cross_dot(top, a_ref[...], MK).astype(bf16)
    both = cross_dot(z, c_ref[...])
    outs[1][...] = both[NB:].astype(bf16)
    outs[2][...] = -both[:NB]


def cross_dot(a, b, dims=KM):
    if b.dtype == bf16:
        return mm(a[0], b, dims) + mm(a[1], b, dims)
    return split_dot(a, halves(b), dims)


def terms(sid, x, a, c):
    size = x.shape[0]
    term = jax.ShapeDtypeStruct((NB, size), bf16)
    return pl.pallas_call(
        terms_kernel,
        out_shape=(term, term, jax.ShapeDtypeStruct((NB, size), f32)),
        in_specs=[SMEM] + [VMEM] * 3,
        out_specs=(VMEM,) * 3,
        compiler_params=PARAMS,
        cost_estimate=pl.CostEstimate(flops=4 * size**3, bytes_accessed=16 * size * size, transcendentals=0),
        name="terms",
    )(sid, x, a, c)


def coupling_kernel(x_ref, a_ref, c_ref, n_ref):
    x = halves(x_ref[...])
    if a_ref.dtype == bf16:
        z = mm(a_ref[...], x[0]) + mm(a_ref[...], x[1])
    else:
        z = split_dot(halves(a_ref[...]), x)
    n_ref[...] = -cross_dot(halves(z), c_ref[...])


def coupled(x, a, c):
    size = x.shape[0]
    return pl.pallas_call(
        coupling_kernel,
        out_shape=jax.ShapeDtypeStruct(x.shape, f32),
        in_specs=[VMEM] * 3,
        out_specs=VMEM,
        compiler_params=PARAMS,
        cost_estimate=pl.CostEstimate(flops=12 * size**3, bytes_accessed=16 * size * size, transcendentals=0),
        name="coupling",
    )(x, a, c)


def passed_along(block, axis, distance, around=False):
    count = lax.axis_size(axis)
    route = [(i, (i + distance) % count) for i in range(count) if around or 0 <= i + distance < count]
    return lax.ppermute(block, axis, route)


def exchanged(blocks):
    return lax.all_to_all(blocks, "swath", 0, 0, tiled=True)


def shards(design, process, prior_prec, routes, counts):
    row_count, size = process.shape[1:]
    swaths = lax.axis_size("swath")
    me = lax.axis_index("tm")
    sid = lax.axis_index("swath")
    total_slots = design.shape[1] * swaths
    ids = jnp.concatenate([me[None].astype(jnp.int32), counts[0], routes[0]])
    sids = sid[None].astype(jnp.int32)
    half = design.shape[1] // 2
    own, ahead = pl.pallas_call(
        functools.partial(weigh_kernel, total_slots),
        out_shape=(
            jax.ShapeDtypeStruct((half, size), bf16),
            jax.ShapeDtypeStruct((half + row_count, size), bf16),
        ),
        in_specs=[SMEM] + [VMEM] * 2,
        out_specs=(VMEM, VMEM),
        compiler_params=PARAMS,
        name="weigh",
    )(ids, design[0], process[0])
    incoming = passed_along(ahead, "tm", 1)
    cut = jax.ShapeDtypeStruct((2 * NB + HALF, NB), f32)
    cuts = jax.ShapeDtypeStruct((swaths,) + cut.shape, f32)
    parts = pl.pallas_call(
        gram_kernel,
        out_shape=cuts,
        in_specs=[VMEM] * 2,
        out_specs=VMEM,
        compiler_params=PARAMS,
        name="gram",
    )(own, incoming)
    diag, copies = pl.pallas_call(
        start_kernel,
        out_shape=(cut, cuts),
        in_specs=[SMEM] + [VMEM] * 4,
        out_specs=(VMEM, VMEM),
        compiler_params=PARAMS,
        name="start",
    )(sids, exchanged(parts), process[0], incoming, prior_prec)
    pair = jnp.concatenate([incoming[half:], process[0]], axis=0)
    pairs = jnp.broadcast_to(pair[None], (swaths,) + pair.shape)
    copies, pairs = lax.optimization_barrier((copies, pairs))
    all_diag = exchanged(copies)
    pairs = exchanged(pairs)
    (x,) = inverse(sids, all_diag)
    a = pairs[:, :row_count].reshape(size, size)
    c = pairs[:, row_count:].reshape(size, size)
    rows = None
    for level in range(LEVELS):
        distance = 2**level
        if level == LEVELS - 1:
            out = terms(sids, x, a, c)
            from_right = passed_along(out[0], "tm", -distance)
            from_left = passed_along(out[1], "tm", distance)
            coupling = passed_along(out[2], "tm", -distance)
            return ((rows - from_left.astype(f32) - from_right.astype(f32))[None], coupling[None])
        right_term, left_term = sliced_terms(sids, x, a, c)
        from_right = passed_along(right_term, "tm", -distance)
        from_left = passed_along(left_term, "tm", distance)
        n = coupled(x, a, c)
        from_right, from_left, n = lax.optimization_barrier((from_right, from_left, n))
        diag, copies = pl.pallas_call(
            next_kernel,
            out_shape=(cut, cuts),
            in_specs=[VMEM] * 3,
            out_specs=(VMEM, VMEM),
            compiler_params=PARAMS,
            name="next",
        )(diag, from_left, from_right)
        x, *tail = inverse(sids, exchanged(copies), level == LEVELS - 2)
        rows = tail[0] if tail else None
        a = passed_along(n, "tm", distance)
        c = passed_along(n, "tm", -distance)


def solution(mesh):
    return jax.shard_map(
        shards,
        mesh=mesh,
        in_specs=(
            P("tm", "swath", None),
            P("tm", "swath", None),
            P("tm", "swath"),
            P("tm", "swath"),
            P("tm", "swath"),
        ),
        out_specs=(P("tm", "swath", None), P("tm", "swath", None)),
        check_vma=False,
    )
```

```python
import functools
import jax
import jax.numpy as jnp
from jax import lax
from jax.experimental import pallas as pl
from jax.experimental.pallas import tpu as pltpu
from jax.sharding import PartitionSpec as P

LEVELS = 3
NB = 128
WIDTH = 16
HALF = NB // 2
f32, bf16 = jnp.float32, jnp.bfloat16
VMEM = pl.BlockSpec(memory_space=pltpu.VMEM)
SMEM = pl.BlockSpec(memory_space=pltpu.SMEM)
PARAMS = pltpu.CompilerParams(vmem_limit_bytes=48 * 2**20)
KK, KM, MK = ((0,), (0,)), ((1,), (0,)), ((1,), (1,))


def mm(a, b, dims=KM):
    return lax.dot_general(a, b, (dims, ((), ())), preferred_element_type=f32)


def halves(x):
    high = x.astype(bf16)
    return high, (x - high.astype(f32)).astype(bf16)


def thirds(x):
    high = x.astype(bf16).astype(f32)
    rest = x - high
    mid = rest.astype(bf16).astype(f32)
    return high, mid, rest - mid


def split_dot(a, b, dims=KM):
    return mm(a[0], b[0], dims) + (mm(a[0], b[1], dims) + mm(a[1], b[0], dims))


def block_inverse(a):
    lane = lax.broadcasted_iota(jnp.int32, (WIDTH, NB), 1)
    row = lax.broadcasted_iota(jnp.int32, (WIDTH, NB), 0)
    lane_all = lax.broadcasted_iota(jnp.int32, (NB, NB), 1)
    p = a[:WIDTH, :]
    for start in range(0, NB, WIDTH):
        stop = start + WIDTH
        inside = (lane >= start) & (lane < stop)
        cols = [jnp.broadcast_to(p[:, start + j : start + j + 1], (WIDTH, NB)) for j in range(WIDTH)]
        h, m, l = thirds(jnp.where(inside, 0.0, jnp.where(lane < start, -p, p)))
        lhs = jnp.concatenate([h, h, m, h, l, m], axis=0).T.astype(bf16)
        x = jnp.where(inside, jnp.where(lane - start == row, 1.0, 0.0), p)
        if stop < NB:
            after = a[stop : stop + WIDTH, :]
            weights = [jnp.broadcast_to(after[:, start + j : start + j + 1], (WIDTH, NB)) for j in range(WIDTH)]
        scale = 1.0 / cols[0][:1, :]
        for j in range(WIDTH):
            c = cols[j]
            now, here = scale, row == j
            if j + 1 < WIDTH:
                pivot = cols[j + 1][j + 1 : j + 2, :] - (c[j + 1 : j + 2, :] * cols[j + 1][j : j + 1, :]) * now
                scale = 1.0 / pivot

            def step(v):
                t = v[j : j + 1, :] * now
                return jnp.where(here, t, v - c * t)

            for i in range(j + 1, WIDTH):
                cols[i] = step(cols[i])
            x = step(x)
        if stop < NB:
            sums = [weights[j] * x[j : j + 1, :] for j in range(4)]
            for j in range(4, WIDTH):
                sums[j % 4] = sums[j % 4] + weights[j] * x[j : j + 1, :]
            p = jnp.where(inside, 0.0, after) - ((sums[0] + sums[1]) + (sums[2] + sums[3]))
        h, m, l = thirds(x)
        rhs = jnp.concatenate([h, m, h, l, h, m], axis=0).astype(bf16)
        a = jnp.where((lane_all >= start) & (lane_all < stop), 0.0, a) - mm(lhs, rhs)
        rows = [x]
        if start:
            rows = [a[:start]] + rows
        if stop < NB:
            rows = rows + [a[stop:]]
        a = jnp.concatenate(rows, axis=0)
    return a


def inverse_kernel(with_rows, sid_ref, g_ref, x_ref, *rest):
    size = x_ref.shape[0]
    count = size // NB
    for k in range(count):
        s, n = slice(k * NB, (k + 1) * NB), (k + 1) % count
        t = slice(n * NB, (n + 1) * NB)
        x_ref[s, s] = g_ref[k, :NB, :]
        block = g_ref[k, NB : 2 * NB, :]
        x_ref[s, t] = block
        x_ref[t, s] = block.T
    for p in range(2):
        s, t = slice(p * NB, (p + 1) * NB), slice((p + 2) * NB, (p + 3) * NB)
        block = jnp.concatenate([g_ref[p, 2 * NB :, :], g_ref[p + 2, 2 * NB :, :]], axis=0)
        x_ref[s, t] = block
        x_ref[t, s] = block.T
    if with_rows:
        rest[0][...] = x_ref[pl.ds(pl.multiple_of(sid_ref[0] * NB, NB), NB), :]
    left_t = rest[-1]
    lane = lax.broadcasted_iota(jnp.int32, (NB, size), 1)

    def eliminate(b, carry):
        first = pl.multiple_of(b * NB, NB)
        at = pl.ds(first, NB)
        inv = block_inverse(x_ref[at, at])
        rows = x_ref[at, :]
        inside = (lane >= first) & (lane < first + NB)
        left_t[...] = jnp.where(lane < first, -rows, rows).T
        w = split_dot(halves(inv), halves(jnp.where(inside, 0.0, rows)))
        w = jnp.where(inside, jnp.concatenate([inv] * count, axis=1), w)
        w_halves = halves(w)
        for i in range(1, count):
            other = pl.ds(pl.multiple_of(lax.rem(b + i, count) * NB, NB), NB)
            x_ref[other, :] = jnp.where(inside, 0.0, x_ref[other, :]) - split_dot(halves(left_t[other, :]), w_halves)
        x_ref[at, :] = w
        return carry

    lax.fori_loop(0, count, eliminate, 0)


def inverse(sid, g, with_rows=False):
    size = 4 * NB
    outs = [jax.ShapeDtypeStruct((size, size), f32)]
    if with_rows:
        outs.append(jax.ShapeDtypeStruct((NB, size), f32))
    return pl.pallas_call(
        functools.partial(inverse_kernel, with_rows),
        out_shape=outs,
        in_specs=[SMEM, VMEM],
        out_specs=[VMEM] * len(outs),
        scratch_shapes=[pltpu.VMEM((size, NB), f32)],
        compiler_params=PARAMS,
        cost_estimate=pl.CostEstimate(flops=60 * size**3, bytes_accessed=8 * size * size, transcendentals=0),
        name="inverse",
    )(sid, g)


def weigh_kernel(total_slots, ids_ref, design_ref, process_ref, own_ref, ahead_ref):
    rows = own_ref.shape[0] // 2
    me, live_count = ids_ref[0], ids_ref[1]
    own_seen = jnp.int32(0)
    for r in range(4):
        target = ids_ref[2 + r]
        is_own = target == me
        live = (r < live_count) & (is_own | (target == me + 1))
        h = design_ref[r * rows : (r + 1) * rows, :].astype(f32)
        mean_sq = jnp.mean(h * h, axis=-1, keepdims=True)
        w = h * lax.rsqrt(4.0 * total_slots * (mean_sq + 1e-06))
        w = jnp.where(live, w, 0.0).astype(bf16)
        ahead_seen = r - own_seen

        @pl.when(is_own)
        def _():
            own_ref[pl.ds(jnp.minimum(own_seen, 1) * rows, rows), :] = w

        @pl.when(jnp.logical_not(is_own))
        def _():
            ahead_ref[pl.ds(jnp.minimum(ahead_seen, 1) * rows, rows), :] = w

        own_seen = own_seen + jnp.where(is_own, 1, 0)
    ahead_ref[2 * rows :, :] = process_ref[...]


def gram_kernel(own_ref, incoming_ref, process_ref, out_ref, pairs_ref):
    both = jnp.concatenate([own_ref[...], incoming_ref[: own_ref.shape[0], :]], axis=0)
    g = mm(both, both, KK)
    for k in range(4):
        n, p, h = (k + 1) % 4, k % 2, HALF * (k // 2)
        out_ref[k, :NB, :] = g[k * NB : (k + 1) * NB, k * NB : (k + 1) * NB]
        out_ref[k, NB : 2 * NB, :] = g[k * NB : (k + 1) * NB, n * NB : (n + 1) * NB]
        pairs_ref[k, :NB, :] = incoming_ref[own_ref.shape[0] :, :]
        pairs_ref[k, NB:, :] = process_ref[...]
        out_ref[k, 2 * NB :, :] = g[p * NB + h : p * NB + h + HALF, (p + 2) * NB : (p + 3) * NB]


def start_kernel(sid_ref, parts_ref, own_ref, incoming_ref, prior_ref, d_ref, copies_ref):
    q = sid_ref[0]
    rows = own_ref[...].astype(f32) + incoming_ref[incoming_ref.shape[0] - NB :, :].astype(f32)
    total = (parts_ref[0] + parts_ref[1]) + (parts_ref[2] + parts_ref[3])

    def block(k):
        out = rows[:, :NB]
        for j in range(1, 4):
            out = jnp.where(k == j, rows[:, j * NB : (j + 1) * NB], out)
        return out

    unit = lax.broadcasted_iota(jnp.int32, (NB, NB), 0) == lax.broadcasted_iota(jnp.int32, (NB, NB), 1)
    across = block(lax.rem(q + 2, 4))
    half = jnp.where(q < 2, across[:HALF, :], across.T[HALF:, :])
    d = jnp.concatenate(
        [
            total[:NB] + (block(q) + jnp.where(unit, prior_ref[...], 0.0)),
            total[NB : 2 * NB] + block(lax.rem(q + 1, 4)),
            total[2 * NB :] + half,
        ],
        axis=0,
    )
    d_ref[...] = d
    for k in range(4):
        copies_ref[k] = d


def next_kernel(d_in, left_ref, right_ref, d_ref, copies_ref):
    d = d_in[...] - left_ref[...] - right_ref[...]
    d_ref[...] = d
    for k in range(4):
        copies_ref[k] = d


def sliced_terms_kernel(sid_ref, x_ref, a_ref, c_ref, right_term, left_term, lhs, flipped):
    q = sid_ref[0]
    p, h = lax.rem(q, 2), pl.multiple_of(lax.div(q, 2) * HALF, HALF)

    def at(k):
        return pl.ds(pl.multiple_of(k * NB, NB), NB)

    own, after, across = at(q), at(lax.rem(q + 1, 4)), at(p + 2)
    lhs[:NB, :] = a_ref[own, :].astype(f32)
    lhs[NB : NB + HALF, :] = a_ref[pl.ds(pl.multiple_of(p * NB + h, HALF), HALF), :].astype(f32)
    lhs[NB + HALF : 2 * NB + HALF, :] = c_ref[:, own].astype(f32).T
    flipped[...] = c_ref[:, at(p)].astype(f32).T
    lhs[2 * NB + HALF :, :] = flipped[pl.ds(h, HALF), :]
    z = halves(split_dot(halves(lhs[...]), halves(x_ref[...])))

    def rows(first, count):
        return z[0][first : first + count], z[1][first : first + count]

    full, part = rows(0, NB), rows(NB, HALF)
    right_term[:NB, :] = cross_dot(full, a_ref[own, :], MK)
    right_term[NB : 2 * NB, :] = cross_dot(full, a_ref[after, :], MK)
    right_term[2 * NB :, :] = cross_dot(part, a_ref[across, :], MK)
    full, part = rows(NB + HALF, NB), rows(2 * NB + HALF, HALF)
    left_term[:NB, :] = cross_dot(full, c_ref[:, own])
    left_term[NB : 2 * NB, :] = cross_dot(full, c_ref[:, after])
    left_term[2 * NB :, :] = cross_dot(part, c_ref[:, across])


def sliced_terms(sid, x, a, c):
    size = x.shape[0]
    out = jax.ShapeDtypeStruct((2 * NB + HALF, NB), f32)
    return pl.pallas_call(
        sliced_terms_kernel,
        out_shape=(out, out),
        in_specs=[SMEM] + [VMEM] * 3,
        out_specs=(VMEM, VMEM),
        scratch_shapes=[pltpu.VMEM((3 * NB, size), f32), pltpu.VMEM((NB, size), f32)],
        compiler_params=PARAMS,
        cost_estimate=pl.CostEstimate(flops=4 * size**3, bytes_accessed=16 * size * size, transcendentals=0),
        name="sliced_terms",
    )(sid, x, a, c)


def row_terms_kernel(sid_ref, x_ref, a_ref, c_ref, right_term, left_term):
    col = pl.multiple_of(sid_ref[0] * NB, NB)
    lhs = jnp.concatenate([a_ref[pl.ds(col, NB), :], c_ref[:, pl.ds(col, NB)].T], axis=0)
    z = halves(split_dot(halves(lhs), halves(x_ref[...])))
    right_term[...] = cross_dot((z[0][:NB], z[1][:NB]), a_ref[...], MK).astype(bf16)
    left_term[...] = cross_dot((z[0][NB:], z[1][NB:]), c_ref[...]).astype(bf16)


def row_coupling_kernel(sid_ref, x_ref, a_ref, c_ref, n_ref):
    rows = a_ref[pl.ds(pl.multiple_of(sid_ref[0] * NB, NB), NB), :]
    z = split_dot(halves(rows), halves(x_ref[...]))
    n_ref[...] = cross_dot(halves(z), c_ref[...])


def negate_kernel(n_ref, out_ref):
    out_ref[...] = -n_ref[...]


def cross_dot(a, b, dims=KM):
    if b.dtype == bf16:
        return mm(a[0], b, dims) + mm(a[1], b, dims)
    return split_dot(a, halves(b), dims)


def row_call(kernel, kinds, sid, x, a, c, name):
    size = x.shape[0]
    return pl.pallas_call(
        kernel,
        out_shape=[jax.ShapeDtypeStruct((NB, size), kind) for kind in kinds],
        in_specs=[SMEM] + [VMEM] * 3,
        out_specs=[VMEM] * len(kinds),
        compiler_params=PARAMS,
        cost_estimate=pl.CostEstimate(flops=8 * size**3, bytes_accessed=16 * size * size, transcendentals=0),
        name=name,
    )(sid, x, a, c)


def coupling_kernel(x_ref, a_ref, c_ref, n_ref):
    x = halves(x_ref[...])
    if a_ref.dtype == bf16:
        z = mm(a_ref[...], x[0]) + mm(a_ref[...], x[1])
    else:
        z = split_dot(halves(a_ref[...]), x)
    n_ref[...] = -cross_dot(halves(z), c_ref[...])


def coupled(x, a, c):
    size = x.shape[0]
    return pl.pallas_call(
        coupling_kernel,
        out_shape=jax.ShapeDtypeStruct(x.shape, f32),
        in_specs=[VMEM] * 3,
        out_specs=VMEM,
        compiler_params=PARAMS,
        cost_estimate=pl.CostEstimate(flops=12 * size**3, bytes_accessed=16 * size * size, transcendentals=0),
        name="coupling",
    )(x, a, c)


def passed_along(block, axis, distance, around=False):
    count = lax.axis_size(axis)
    route = [(i, (i + distance) % count) for i in range(count) if around or 0 <= i + distance < count]
    return lax.ppermute(block, axis, route)


def exchanged(blocks):
    return lax.all_to_all(blocks, "swath", 0, 0, tiled=True)


def shards(design, process, prior_prec, routes, counts):
    row_count, size = process.shape[1:]
    swaths = lax.axis_size("swath")
    me = lax.axis_index("tm")
    sid = lax.axis_index("swath")
    total_slots = design.shape[1] * swaths
    ids = jnp.concatenate([me[None].astype(jnp.int32), counts[0], routes[0]])
    sids = sid[None].astype(jnp.int32)
    half = design.shape[1] // 2
    own, ahead = pl.pallas_call(
        functools.partial(weigh_kernel, total_slots),
        out_shape=(
            jax.ShapeDtypeStruct((half, size), bf16),
            jax.ShapeDtypeStruct((half + row_count, size), bf16),
        ),
        in_specs=[SMEM] + [VMEM] * 2,
        out_specs=(VMEM, VMEM),
        compiler_params=PARAMS,
        name="weigh",
    )(ids, design[0], process[0])
    incoming = passed_along(ahead, "tm", 1)
    cut = jax.ShapeDtypeStruct((2 * NB + HALF, NB), f32)
    cuts = jax.ShapeDtypeStruct((swaths,) + cut.shape, f32)
    parts, pairs = pl.pallas_call(
        gram_kernel,
        out_shape=(cuts, jax.ShapeDtypeStruct((swaths, 2 * row_count, size), bf16)),
        in_specs=[VMEM] * 3,
        out_specs=(VMEM, VMEM),
        compiler_params=PARAMS,
        name="gram",
    )(own, incoming, process[0])
    diag, copies = pl.pallas_call(
        start_kernel,
        out_shape=(cut, cuts),
        in_specs=[SMEM] + [VMEM] * 4,
        out_specs=(VMEM, VMEM),
        compiler_params=PARAMS,
        name="start",
    )(sids, exchanged(parts), process[0], incoming, prior_prec)
    copies, pairs = lax.optimization_barrier((copies, pairs))
    all_diag = exchanged(copies)
    pairs = exchanged(pairs)
    (x,) = inverse(sids, all_diag)
    a = pairs[:, :row_count].reshape(size, size)
    c = pairs[:, row_count:].reshape(size, size)
    rows = None
    for level in range(LEVELS):
        distance = 2**level
        if level == LEVELS - 1:
            (n,) = row_call(row_coupling_kernel, (f32,), sids, x, a, c, "row_coupling")
            coupling = passed_along(n, "tm", -distance)
            x, n = lax.optimization_barrier((x, n))
            right_term, left_term = row_call(row_terms_kernel, (bf16, bf16), sids, x, a, c, "row_terms")
            from_right = passed_along(right_term, "tm", -distance)
            from_left = passed_along(left_term, "tm", distance)
            coupling = pl.pallas_call(
                negate_kernel,
                out_shape=jax.ShapeDtypeStruct(coupling.shape, f32),
                in_specs=[VMEM],
                out_specs=VMEM,
                compiler_params=PARAMS,
                cost_estimate=pl.CostEstimate(flops=size * NB, bytes_accessed=8 * size * NB, transcendentals=0),
                name="negate",
            )(coupling)
            rows, coupling = lax.optimization_barrier((rows, coupling))
            return ((rows - from_left.astype(f32) - from_right.astype(f32))[None], coupling[None])
        right_term, left_term = sliced_terms(sids, x, a, c)
        from_right = passed_along(right_term, "tm", -distance)
        from_left = passed_along(left_term, "tm", distance)
        n = coupled(x, a, c)
        from_right, from_left, n = lax.optimization_barrier((from_right, from_left, n))
        diag, copies = pl.pallas_call(
            next_kernel,
            out_shape=(cut, cuts),
            in_specs=[VMEM] * 3,
            out_specs=(VMEM, VMEM),
            compiler_params=PARAMS,
            name="next",
        )(diag, from_left, from_right)
        x, *tail = inverse(sids, exchanged(copies), level == LEVELS - 2)
        rows = tail[0] if tail else None
        a = passed_along(n, "tm", distance)
        c = passed_along(n, "tm", -distance)


def solution(mesh):
    return jax.shard_map(
        shards,
        mesh=mesh,
        in_specs=(
            P("tm", "swath", None),
            P("tm", "swath", None),
            P("tm", "swath"),
            P("tm", "swath"),
            P("tm", "swath"),
        ),
        out_specs=(P("tm", "swath", None), P("tm", "swath", None)),
        check_vma=False,
    )
```

```python
import functools
import jax
import jax.numpy as jnp
from jax import lax
from jax.experimental import pallas as pl
from jax.experimental.pallas import tpu as pltpu
from jax.sharding import PartitionSpec as P

LEVELS = 3
NB = 128
WIDTH = 16
HALF = NB // 2
f32, bf16 = jnp.float32, jnp.bfloat16
VMEM = pl.BlockSpec(memory_space=pltpu.VMEM)
SMEM = pl.BlockSpec(memory_space=pltpu.SMEM)
HBM = pl.BlockSpec(memory_space=pltpu.HBM)
PARAMS = pltpu.CompilerParams(vmem_limit_bytes=48 * 2**20)
KK, KM, MK = ((0,), (0,)), ((1,), (0,)), ((1,), (1,))


def mm(a, b, dims=KM):
    return lax.dot_general(a, b, (dims, ((), ())), preferred_element_type=f32)


def halves(x):
    high = x.astype(bf16)
    return high, (x - high.astype(f32)).astype(bf16)


def thirds(x):
    high = x.astype(bf16).astype(f32)
    rest = x - high
    mid = rest.astype(bf16).astype(f32)
    return high, mid, rest - mid


def split_dot(a, b, dims=KM):
    return mm(a[0], b[0], dims) + (mm(a[0], b[1], dims) + mm(a[1], b[0], dims))


def block_inverse(a):
    lane = lax.broadcasted_iota(jnp.int32, (WIDTH, NB), 1)
    row = lax.broadcasted_iota(jnp.int32, (WIDTH, NB), 0)
    lane_all = lax.broadcasted_iota(jnp.int32, (NB, NB), 1)
    p = a[:WIDTH, :]
    for start in range(0, NB, WIDTH):
        stop = start + WIDTH
        inside = (lane >= start) & (lane < stop)
        cols = [jnp.broadcast_to(p[:, start + j : start + j + 1], (WIDTH, NB)) for j in range(WIDTH)]
        h, m, l = thirds(jnp.where(inside, 0.0, jnp.where(lane < start, -p, p)))
        lhs = jnp.concatenate([h, h, m, h, l, m], axis=0).T.astype(bf16)
        x = jnp.where(inside, jnp.where(lane - start == row, 1.0, 0.0), p)
        if stop < NB:
            after = a[stop : stop + WIDTH, :]
            weights = [jnp.broadcast_to(after[:, start + j : start + j + 1], (WIDTH, NB)) for j in range(WIDTH)]
        scale = 1.0 / cols[0][:1, :]
        for j in range(WIDTH):
            c = cols[j]
            now, here = scale, row == j
            if j + 1 < WIDTH:
                pivot = cols[j + 1][j + 1 : j + 2, :] - (c[j + 1 : j + 2, :] * cols[j + 1][j : j + 1, :]) * now
                scale = 1.0 / pivot

            def step(v):
                t = v[j : j + 1, :] * now
                return jnp.where(here, t, v - c * t)

            for i in range(j + 1, WIDTH):
                cols[i] = step(cols[i])
            x = step(x)
        if stop < NB:
            sums = [weights[j] * x[j : j + 1, :] for j in range(4)]
            for j in range(4, WIDTH):
                sums[j % 4] = sums[j % 4] + weights[j] * x[j : j + 1, :]
            p = jnp.where(inside, 0.0, after) - ((sums[0] + sums[1]) + (sums[2] + sums[3]))
        h, m, l = thirds(x)
        rhs = jnp.concatenate([h, m, h, l, h, m], axis=0).astype(bf16)
        a = jnp.where((lane_all >= start) & (lane_all < stop), 0.0, a) - mm(lhs, rhs)
        rows = [x]
        if start:
            rows = [a[:start]] + rows
        if stop < NB:
            rows = rows + [a[stop:]]
        a = jnp.concatenate(rows, axis=0)
    return a


def inverse_kernel(with_rows, sid_ref, g_ref, x_ref, *rest):
    size = x_ref.shape[0]
    count = size // NB
    for k in range(count):
        s, n = slice(k * NB, (k + 1) * NB), (k + 1) % count
        t = slice(n * NB, (n + 1) * NB)
        x_ref[s, s] = g_ref[k, :NB, :]
        block = g_ref[k, NB : 2 * NB, :]
        x_ref[s, t] = block
        x_ref[t, s] = block.T
    for p in range(2):
        s, t = slice(p * NB, (p + 1) * NB), slice((p + 2) * NB, (p + 3) * NB)
        block = jnp.concatenate([g_ref[p, 2 * NB :, :], g_ref[p + 2, 2 * NB :, :]], axis=0)
        x_ref[s, t] = block
        x_ref[t, s] = block.T
    if with_rows:
        rest[0][...] = x_ref[pl.ds(pl.multiple_of(sid_ref[0] * NB, NB), NB), :]
    left_t = rest[-1]
    lane = lax.broadcasted_iota(jnp.int32, (NB, size), 1)

    def eliminate(b, carry):
        first = pl.multiple_of(b * NB, NB)
        at = pl.ds(first, NB)
        inv = block_inverse(x_ref[at, at])
        rows = x_ref[at, :]
        inside = (lane >= first) & (lane < first + NB)
        left_t[...] = jnp.where(lane < first, -rows, rows).T
        w = split_dot(halves(inv), halves(jnp.where(inside, 0.0, rows)))
        w = jnp.where(inside, jnp.concatenate([inv] * count, axis=1), w)
        w_halves = halves(w)
        for i in range(1, count):
            other = pl.ds(pl.multiple_of(lax.rem(b + i, count) * NB, NB), NB)
            x_ref[other, :] = jnp.where(inside, 0.0, x_ref[other, :]) - split_dot(halves(left_t[other, :]), w_halves)
        x_ref[at, :] = w
        return carry

    lax.fori_loop(0, count, eliminate, 0)


def inverse(sid, g, with_rows=False):
    size = 4 * NB
    outs = [jax.ShapeDtypeStruct((size, size), f32)]
    if with_rows:
        outs.append(jax.ShapeDtypeStruct((NB, size), f32))
    return pl.pallas_call(
        functools.partial(inverse_kernel, with_rows),
        out_shape=outs,
        in_specs=[SMEM, VMEM],
        out_specs=[VMEM] * len(outs),
        scratch_shapes=[pltpu.VMEM((size, NB), f32)],
        compiler_params=PARAMS,
        cost_estimate=pl.CostEstimate(flops=40*size**3 if with_rows else 60 * size**3, bytes_accessed=8 * size * size, transcendentals=0),
        name="inverse",
    )(sid, g)


def weigh_kernel(total_slots, counts_ref, routes_ref, design_hbm, process_hbm, own_ref, ahead_ref, design_ref, process_ref, sems):
    rows = own_ref.shape[0] // 2
    loads = [
        pltpu.make_async_copy(design_hbm.at[0], design_ref, sems.at[0]),
        pltpu.make_async_copy(process_hbm.at[0], process_ref, sems.at[1]),
    ]
    for load in loads:
        load.start()
    me, live_count = lax.axis_index("tm"), counts_ref[0, 0]
    loads[0].wait()
    own_seen = jnp.int32(0)
    for r in range(4):
        target = routes_ref[0, r]
        is_own = target == me
        live = (r < live_count) & (is_own | (target == me + 1))
        h = design_ref[r * rows : (r + 1) * rows, :].astype(f32)
        mean_sq = jnp.mean(h * h, axis=-1, keepdims=True)
        w = h * lax.rsqrt(4.0 * total_slots * (mean_sq + 1e-06))
        w = jnp.where(live, w, 0.0).astype(bf16)
        ahead_seen = r - own_seen

        @pl.when(is_own)
        def _():
            own_ref[pl.ds(jnp.minimum(own_seen, 1) * rows, rows), :] = w

        @pl.when(jnp.logical_not(is_own))
        def _():
            ahead_ref[pl.ds(jnp.minimum(ahead_seen, 1) * rows, rows), :] = w

        own_seen = own_seen + jnp.where(is_own, 1, 0)
    loads[1].wait()
    ahead_ref[2 * rows :, :] = process_ref[...]


def gram_kernel(own_ref, incoming_ref, process_ref, out_ref, pairs_ref):
    both = jnp.concatenate([own_ref[...], incoming_ref[: own_ref.shape[0], :]], axis=0)
    g = mm(both, both, KK)
    for k in range(4):
        n, p, h = (k + 1) % 4, k % 2, HALF * (k // 2)
        out_ref[k, :NB, :] = g[k * NB : (k + 1) * NB, k * NB : (k + 1) * NB]
        out_ref[k, NB : 2 * NB, :] = g[k * NB : (k + 1) * NB, n * NB : (n + 1) * NB]
        pairs_ref[k, :NB, :] = incoming_ref[own_ref.shape[0] :, :]
        pairs_ref[k, NB:, :] = process_ref[...]
        out_ref[k, 2 * NB :, :] = g[p * NB + h : p * NB + h + HALF, (p + 2) * NB : (p + 3) * NB]


def start_kernel(sid_ref, parts_ref, own_ref, incoming_ref, prior_ref, d_ref, copies_ref):
    q = sid_ref[0]
    rows = own_ref[...].astype(f32) + incoming_ref[incoming_ref.shape[0] - NB :, :].astype(f32)
    total = (parts_ref[0] + parts_ref[1]) + (parts_ref[2] + parts_ref[3])

    def block(k):
        out = rows[:, :NB]
        for j in range(1, 4):
            out = jnp.where(k == j, rows[:, j * NB : (j + 1) * NB], out)
        return out

    unit = lax.broadcasted_iota(jnp.int32, (NB, NB), 0) == lax.broadcasted_iota(jnp.int32, (NB, NB), 1)
    across = block(lax.rem(q + 2, 4))
    half = jnp.where(q < 2, across[:HALF, :], across.T[HALF:, :])
    d = jnp.concatenate(
        [
            total[:NB] + (block(q) + jnp.where(unit, prior_ref[...], 0.0)),
            total[NB : 2 * NB] + block(lax.rem(q + 1, 4)),
            total[2 * NB :] + half,
        ],
        axis=0,
    )
    d_ref[...] = d
    for k in range(4):
        copies_ref[k] = d


def next_kernel(d_in, left_ref, right_ref, d_ref, copies_ref):
    d = d_in[...] - left_ref[...] - right_ref[...]
    d_ref[...] = d
    for k in range(4):
        copies_ref[k] = d


def sliced_terms_kernel(sid_ref, x_ref, a_ref, c_ref, right_term, left_term, lhs, flipped):
    q = sid_ref[0]
    p, h = lax.rem(q, 2), pl.multiple_of(lax.div(q, 2) * HALF, HALF)

    def at(k):
        return pl.ds(pl.multiple_of(k * NB, NB), NB)

    own, after, across = at(q), at(lax.rem(q + 1, 4)), at(p + 2)
    lhs[:NB, :] = a_ref[own, :].astype(f32)
    lhs[NB : NB + HALF, :] = a_ref[pl.ds(pl.multiple_of(p * NB + h, HALF), HALF), :].astype(f32)
    lhs[NB + HALF : 2 * NB + HALF, :] = c_ref[:, own].astype(f32).T
    flipped[...] = c_ref[:, at(p)].astype(f32).T
    lhs[2 * NB + HALF :, :] = flipped[pl.ds(h, HALF), :]
    z = halves(split_dot(halves(lhs[...]), halves(x_ref[...])))

    def rows(first, count):
        return z[0][first : first + count], z[1][first : first + count]

    full, part = rows(0, NB), rows(NB, HALF)
    right_term[:NB, :] = cross_dot(full, a_ref[own, :], MK)
    right_term[NB : 2 * NB, :] = cross_dot(full, a_ref[after, :], MK)
    right_term[2 * NB :, :] = cross_dot(part, a_ref[across, :], MK)
    full, part = rows(NB + HALF, NB), rows(2 * NB + HALF, HALF)
    left_term[:NB, :] = cross_dot(full, c_ref[:, own])
    left_term[NB : 2 * NB, :] = cross_dot(full, c_ref[:, after])
    left_term[2 * NB :, :] = cross_dot(part, c_ref[:, across])


def sliced_terms(sid, x, a, c):
    size = x.shape[0]
    out = jax.ShapeDtypeStruct((2 * NB + HALF, NB), f32)
    return pl.pallas_call(
        sliced_terms_kernel,
        out_shape=(out, out),
        in_specs=[SMEM] + [VMEM] * 3,
        out_specs=(VMEM, VMEM),
        scratch_shapes=[pltpu.VMEM((3 * NB, size), f32), pltpu.VMEM((NB, size), f32)],
        compiler_params=PARAMS,
        cost_estimate=pl.CostEstimate(flops=4 * size**3, bytes_accessed=16 * size * size, transcendentals=0),
        name="sliced_terms",
    )(sid, x, a, c)


def row_terms_kernel(sid_ref, x_ref, a_ref, c_ref, right_term, left_term):
    col = pl.multiple_of(sid_ref[0] * NB, NB)
    lhs = jnp.concatenate([a_ref[pl.ds(col, NB), :], c_ref[:, pl.ds(col, NB)].T], axis=0)
    z = halves(split_dot(halves(lhs), halves(x_ref[...])))
    right_term[...] = cross_dot((z[0][:NB], z[1][:NB]), a_ref[...], MK).astype(bf16)
    left_term[...] = cross_dot((z[0][NB:], z[1][NB:]), c_ref[...]).astype(bf16)


def row_coupling_kernel(sid_ref, x_ref, a_ref, c_ref, n_ref):
    rows = a_ref[pl.ds(pl.multiple_of(sid_ref[0] * NB, NB), NB), :]
    z = split_dot(halves(rows), halves(x_ref[...]))
    n_ref[...] = cross_dot(halves(z), c_ref[...])


def negate_kernel(n_ref, out_ref):
    out_ref[...] = -n_ref[...]


def cross_dot(a, b, dims=KM):
    if b.dtype == bf16:
        return mm(a[0], b, dims) + mm(a[1], b, dims)
    return split_dot(a, halves(b), dims)


def row_call(kernel, kinds, sid, x, a, c, name):
    size = x.shape[0]
    return pl.pallas_call(
        kernel,
        out_shape=[jax.ShapeDtypeStruct((NB, size), kind) for kind in kinds],
        in_specs=[SMEM] + [VMEM] * 3,
        out_specs=[VMEM] * len(kinds),
        compiler_params=PARAMS,
        cost_estimate=pl.CostEstimate(flops=8 * size**3, bytes_accessed=16 * size * size, transcendentals=0),
        name=name,
    )(sid, x, a, c)


def coupling_kernel(x_ref, a_ref, c_ref, n_ref):
    x = halves(x_ref[...])
    if a_ref.dtype == bf16:
        z = mm(a_ref[...], x[0]) + mm(a_ref[...], x[1])
    else:
        z = split_dot(halves(a_ref[...]), x)
    n_ref[...] = -cross_dot(halves(z), c_ref[...])


def coupled(x, a, c):
    size = x.shape[0]
    return pl.pallas_call(
        coupling_kernel,
        out_shape=jax.ShapeDtypeStruct(x.shape, f32),
        in_specs=[VMEM] * 3,
        out_specs=VMEM,
        compiler_params=PARAMS,
        cost_estimate=pl.CostEstimate(flops=12 * size**3, bytes_accessed=16 * size * size, transcendentals=0),
        name="coupling",
    )(x, a, c)


def passed_along(block, axis, distance, around=False):
    count = lax.axis_size(axis)
    route = [(i, (i + distance) % count) for i in range(count) if around or 0 <= i + distance < count]
    return lax.ppermute(block, axis, route)


def exchanged(blocks):
    return lax.all_to_all(blocks, "swath", 0, 0, tiled=True)


def shards(design, process, prior_prec, routes, counts):
    row_count, size = process.shape[1:]
    swaths = lax.axis_size("swath")
    sid = lax.axis_index("swath")
    total_slots = design.shape[1] * swaths
    sids = sid[None].astype(jnp.int32)
    half = design.shape[1] // 2
    own, ahead = pl.pallas_call(
        functools.partial(weigh_kernel, total_slots),
        out_shape=(
            jax.ShapeDtypeStruct((half, size), bf16),
            jax.ShapeDtypeStruct((half + row_count, size), bf16),
        ),
        in_specs=[SMEM, SMEM, HBM, HBM],
        out_specs=(VMEM, VMEM),
        scratch_shapes=[pltpu.VMEM((design.shape[1], size), bf16), pltpu.VMEM((row_count, size), bf16), pltpu.SemaphoreType.DMA((2,))],
        compiler_params=pltpu.CompilerParams(vmem_limit_bytes=63 * 2**20),
        name="weigh",
    )(counts, routes, design, process)
    incoming = passed_along(ahead, "tm", 1)
    cut = jax.ShapeDtypeStruct((2 * NB + HALF, NB), f32)
    cuts = jax.ShapeDtypeStruct((swaths,) + cut.shape, f32)
    parts, pairs = pl.pallas_call(
        gram_kernel,
        out_shape=(cuts, jax.ShapeDtypeStruct((swaths, 2 * row_count, size), bf16)),
        in_specs=[VMEM] * 3,
        out_specs=(VMEM, VMEM),
        compiler_params=PARAMS,
        name="gram",
    )(own, incoming, process[0])
    diag, copies = pl.pallas_call(
        start_kernel,
        out_shape=(cut, cuts),
        in_specs=[SMEM] + [VMEM] * 4,
        out_specs=(VMEM, VMEM),
        compiler_params=PARAMS,
        name="start",
    )(sids, exchanged(parts), process[0], incoming, prior_prec)
    copies, pairs = lax.optimization_barrier((copies, pairs))
    all_diag = exchanged(copies)
    pairs = exchanged(pairs)
    (x,) = inverse(sids, all_diag)
    a = pairs[:, :row_count].reshape(size, size)
    c = pairs[:, row_count:].reshape(size, size)
    rows = None
    for level in range(LEVELS):
        distance = 2**level
        if level == LEVELS - 1:
            (n,) = row_call(row_coupling_kernel, (f32,), sids, x, a, c, "row_coupling")
            coupling = passed_along(n, "tm", -distance)
            x, n = lax.optimization_barrier((x, n))
            right_term, left_term = row_call(row_terms_kernel, (bf16, bf16), sids, x, a, c, "row_terms")
            from_right = passed_along(right_term, "tm", -distance)
            from_left = passed_along(left_term, "tm", distance)
            coupling = pl.pallas_call(
                negate_kernel,
                out_shape=jax.ShapeDtypeStruct(coupling.shape, f32),
                in_specs=[VMEM],
                out_specs=VMEM,
                compiler_params=PARAMS,
                cost_estimate=pl.CostEstimate(flops=size * NB, bytes_accessed=8 * size * NB, transcendentals=0),
                name="negate",
            )(coupling)
            rows, coupling = lax.optimization_barrier((rows, coupling))
            return ((rows - from_left.astype(f32) - from_right.astype(f32))[None], coupling[None])
        right_term, left_term = sliced_terms(sids, x, a, c)
        x, right_term, left_term = lax.optimization_barrier((x, right_term, left_term))
        from_right = passed_along(right_term, "tm", -distance)
        from_left = passed_along(left_term, "tm", distance)
        n = coupled(x, a, c)
        from_right, from_left, _ = lax.optimization_barrier((from_right, from_left, n))
        diag, copies = pl.pallas_call(
            next_kernel,
            out_shape=(cut, cuts),
            in_specs=[VMEM] * 3,
            out_specs=(VMEM, VMEM),
            compiler_params=PARAMS,
            name="next",
        )(diag, from_left, from_right)
        x, *tail = inverse(sids, exchanged(copies), level == LEVELS - 2)
        rows = tail[0] if tail else None
        a = passed_along(n, "tm", distance)
        c = passed_along(n, "tm", -distance)


def solution(mesh):
    return jax.shard_map(
        shards,
        mesh=mesh,
        in_specs=(
            P("tm", "swath", None),
            P("tm", "swath", None),
            P("tm", "swath"),
            P("tm", "swath"),
            P("tm", "swath"),
        ),
        out_specs=(P("tm", "swath", None), P("tm", "swath", None)),
        check_vma=False,
    )
```

```python
import functools
import jax
import jax.numpy as jnp
from jax import lax
from jax.experimental import pallas as pl
from jax.experimental.pallas import tpu as pltpu
from jax.sharding import PartitionSpec as P

LEVELS = 3
NB = 128
WIDTH = 16
HALF = NB // 2
f32, bf16 = jnp.float32, jnp.bfloat16
VMEM = pl.BlockSpec(memory_space=pltpu.VMEM)
SMEM = pl.BlockSpec(memory_space=pltpu.SMEM)
HBM = pl.BlockSpec(memory_space=pltpu.HBM)
PARAMS = pltpu.CompilerParams(vmem_limit_bytes=48 * 2**20)
KK, KM, MK = ((0,), (0,)), ((1,), (0,)), ((1,), (1,))


def mm(a, b, dims=KM):
    return lax.dot_general(a, b, (dims, ((), ())), preferred_element_type=f32)


def halves(x):
    high = x.astype(bf16)
    return high, (x - high.astype(f32)).astype(bf16)


def thirds(x):
    high = x.astype(bf16).astype(f32)
    rest = x - high
    mid = rest.astype(bf16).astype(f32)
    return high, mid, rest - mid


def split_dot(a, b, dims=KM):
    return mm(a[0], b[0], dims) + (mm(a[0], b[1], dims) + mm(a[1], b[0], dims))


def block_inverse(a):
    lane = lax.broadcasted_iota(jnp.int32, (WIDTH, NB), 1)
    row = lax.broadcasted_iota(jnp.int32, (WIDTH, NB), 0)
    lane_all = lax.broadcasted_iota(jnp.int32, (NB, NB), 1)
    p = a[:WIDTH, :]
    for start in range(0, NB, WIDTH):
        stop = start + WIDTH
        inside = (lane >= start) & (lane < stop)
        cols = [jnp.broadcast_to(p[:, start + j : start + j + 1], (WIDTH, NB)) for j in range(WIDTH)]
        h, m, l = thirds(jnp.where(inside, 0.0, jnp.where(lane < start, -p, p)))
        lhs = jnp.concatenate([h, h, m, h, l, m], axis=0).T.astype(bf16)
        x = jnp.where(inside, jnp.where(lane - start == row, 1.0, 0.0), p)
        if stop < NB:
            after = a[stop : stop + WIDTH, :]
            weights = [jnp.broadcast_to(after[:, start + j : start + j + 1], (WIDTH, NB)) for j in range(WIDTH)]
        units = [1.0 / cols[j][j : j + 1, :] for j in range(WIDTH)]
        scale = jnp.ones((1, NB), f32)
        for j in range(WIDTH):
            c = cols[j]
            now, here = scale * units[j], row == j
            if j + 1 < WIDTH:
                pair = (c[j + 1 : j + 2, :] * units[j + 1]) * (cols[j + 1][j : j + 1, :] * units[j])
                scale = 1.0 / (cols[j + 1][j + 1 : j + 2, :] * units[j + 1] - pair * scale)

            def step(v):
                t = v[j : j + 1, :] * now
                return jnp.where(here, t, v - c * t)

            for i in range(j + 1, WIDTH):
                cols[i] = step(cols[i])
            x = step(x)
        if stop < NB:
            sums = [weights[j] * x[j : j + 1, :] for j in range(4)]
            for j in range(4, WIDTH):
                sums[j % 4] = sums[j % 4] + weights[j] * x[j : j + 1, :]
            p = jnp.where(inside, 0.0, after) - ((sums[0] + sums[1]) + (sums[2] + sums[3]))
        h, m, l = thirds(x)
        rhs = jnp.concatenate([h, m, h, l, h, m], axis=0).astype(bf16)
        a = jnp.where((lane_all >= start) & (lane_all < stop), 0.0, a) - mm(lhs, rhs)
        rows = [x]
        if start:
            rows = [a[:start]] + rows
        if stop < NB:
            rows = rows + [a[stop:]]
        a = jnp.concatenate(rows, axis=0)
    return a


def inverse_kernel(with_rows, sid_ref, g_ref, x_ref, *rest):
    size = x_ref.shape[0]
    count = size // NB
    for k in range(count):
        s, n = slice(k * NB, (k + 1) * NB), (k + 1) % count
        t = slice(n * NB, (n + 1) * NB)
        x_ref[s, s] = g_ref[k, :NB, :]
        block = g_ref[k, NB : 2 * NB, :]
        x_ref[s, t] = block
        x_ref[t, s] = block.T
    for p in range(2):
        s, t = slice(p * NB, (p + 1) * NB), slice((p + 2) * NB, (p + 3) * NB)
        block = jnp.concatenate([g_ref[p, 2 * NB :, :], g_ref[p + 2, 2 * NB :, :]], axis=0)
        x_ref[s, t] = block
        x_ref[t, s] = block.T
    if with_rows:
        rest[0][...] = x_ref[pl.ds(pl.multiple_of(sid_ref[0] * NB, NB), NB), :]
    left_t = rest[-1]
    lane = lax.broadcasted_iota(jnp.int32, (NB, size), 1)

    def eliminate(b, carry):
        first = pl.multiple_of(b * NB, NB)
        at = pl.ds(first, NB)
        inv = block_inverse(x_ref[at, at])
        rows = x_ref[at, :]
        inside = (lane >= first) & (lane < first + NB)
        left_t[...] = jnp.where(lane < first, -rows, rows).T
        w = split_dot(halves(inv), halves(jnp.where(inside, 0.0, rows)))
        w = jnp.where(inside, jnp.concatenate([inv] * count, axis=1), w)
        w_halves = halves(w)
        for i in range(1, count):
            other = pl.ds(pl.multiple_of(lax.rem(b + i, count) * NB, NB), NB)
            x_ref[other, :] = jnp.where(inside, 0.0, x_ref[other, :]) - split_dot(halves(left_t[other, :]), w_halves)
        x_ref[at, :] = w
        return carry

    lax.fori_loop(0, count, eliminate, 0)


def inverse(sid, g, with_rows=False):
    size = 4 * NB
    outs = [jax.ShapeDtypeStruct((size, size), f32)]
    if with_rows:
        outs.append(jax.ShapeDtypeStruct((NB, size), f32))
    return pl.pallas_call(
        functools.partial(inverse_kernel, with_rows),
        out_shape=outs,
        in_specs=[SMEM, VMEM],
        out_specs=[VMEM] * len(outs),
        scratch_shapes=[pltpu.VMEM((size, NB), f32)],
        compiler_params=PARAMS,
        cost_estimate=pl.CostEstimate(flops=40*size**3 if with_rows else 60 * size**3, bytes_accessed=8 * size * size, transcendentals=0),
        name="inverse",
    )(sid, g)


def weigh_kernel(total_slots, counts_ref, routes_ref, design_hbm, process_hbm, own_ref, ahead_ref, design_ref, process_ref, sems):
    rows = own_ref.shape[0] // 2
    loads = [
        pltpu.make_async_copy(design_hbm.at[0], design_ref, sems.at[0]),
        pltpu.make_async_copy(process_hbm.at[0], process_ref, sems.at[1]),
    ]
    for load in loads:
        load.start()
    me, live_count = lax.axis_index("tm"), counts_ref[0, 0]
    loads[0].wait()
    own_seen = jnp.int32(0)
    for r in range(4):
        target = routes_ref[0, r]
        is_own = target == me
        live = (r < live_count) & (is_own | (target == me + 1))
        h = design_ref[r * rows : (r + 1) * rows, :].astype(f32)
        mean_sq = jnp.mean(h * h, axis=-1, keepdims=True)
        w = h * lax.rsqrt(4.0 * total_slots * (mean_sq + 1e-06))
        w = jnp.where(live, w, 0.0).astype(bf16)
        ahead_seen = r - own_seen

        @pl.when(is_own)
        def _():
            own_ref[pl.ds(jnp.minimum(own_seen, 1) * rows, rows), :] = w

        @pl.when(jnp.logical_not(is_own))
        def _():
            ahead_ref[pl.ds(jnp.minimum(ahead_seen, 1) * rows, rows), :] = w

        own_seen = own_seen + jnp.where(is_own, 1, 0)
    loads[1].wait()
    ahead_ref[2 * rows :, :] = process_ref[...]


def own_gram_kernel(own_ref, g_ref):
    g_ref[...] = mm(own_ref[...], own_ref[...], KK)


def gram_kernel(g_ref, incoming_ref, process_ref, out_ref, pairs_ref):
    half = incoming_ref.shape[0] - NB
    g = g_ref[...] + mm(incoming_ref[:half, :], incoming_ref[:half, :], KK)
    for k in range(4):
        n, p, h = (k + 1) % 4, k % 2, HALF * (k // 2)
        out_ref[k, :NB, :] = g[k * NB : (k + 1) * NB, k * NB : (k + 1) * NB]
        out_ref[k, NB : 2 * NB, :] = g[k * NB : (k + 1) * NB, n * NB : (n + 1) * NB]
        pairs_ref[k, :NB, :] = incoming_ref[half:, :]
        pairs_ref[k, NB:, :] = process_ref[...]
        out_ref[k, 2 * NB :, :] = g[p * NB + h : p * NB + h + HALF, (p + 2) * NB : (p + 3) * NB]


def start_kernel(sid_ref, parts_ref, own_ref, incoming_ref, prior_ref, d_ref, copies_ref):
    q = sid_ref[0]
    rows = own_ref[...].astype(f32) + incoming_ref[incoming_ref.shape[0] - NB :, :].astype(f32)
    total = (parts_ref[0] + parts_ref[1]) + (parts_ref[2] + parts_ref[3])

    def block(k):
        out = rows[:, :NB]
        for j in range(1, 4):
            out = jnp.where(k == j, rows[:, j * NB : (j + 1) * NB], out)
        return out

    unit = lax.broadcasted_iota(jnp.int32, (NB, NB), 0) == lax.broadcasted_iota(jnp.int32, (NB, NB), 1)
    across = block(lax.rem(q + 2, 4))
    half = jnp.where(q < 2, across[:HALF, :], across.T[HALF:, :])
    d = jnp.concatenate(
        [
            total[:NB] + (block(q) + jnp.where(unit, prior_ref[...], 0.0)),
            total[NB : 2 * NB] + block(lax.rem(q + 1, 4)),
            total[2 * NB :] + half,
        ],
        axis=0,
    )
    d_ref[...] = d
    for k in range(4):
        copies_ref[k] = d


def next_kernel(d_in, left_ref, right_ref, d_ref, copies_ref):
    d = d_in[...] - left_ref[...] - right_ref[...]
    d_ref[...] = d
    for k in range(4):
        copies_ref[k] = d


def sliced_terms_kernel(sid_ref, x_ref, a_ref, c_ref, right_term, left_term, lhs, flipped):
    q = sid_ref[0]
    p, h = lax.rem(q, 2), pl.multiple_of(lax.div(q, 2) * HALF, HALF)

    def at(k):
        return pl.ds(pl.multiple_of(k * NB, NB), NB)

    own, after, across = at(q), at(lax.rem(q + 1, 4)), at(p + 2)
    lhs[:NB, :] = a_ref[own, :].astype(f32)
    lhs[NB : NB + HALF, :] = a_ref[pl.ds(pl.multiple_of(p * NB + h, HALF), HALF), :].astype(f32)
    lhs[NB + HALF : 2 * NB + HALF, :] = c_ref[:, own].astype(f32).T
    flipped[...] = c_ref[:, at(p)].astype(f32).T
    lhs[2 * NB + HALF :, :] = flipped[pl.ds(h, HALF), :]
    z = halves(split_dot(halves(lhs[...]), halves(x_ref[...])))

    def rows(first, count):
        return z[0][first : first + count], z[1][first : first + count]

    full, part = rows(0, NB), rows(NB, HALF)
    right_term[:NB, :] = cross_dot(full, a_ref[own, :], MK)
    right_term[NB : 2 * NB, :] = cross_dot(full, a_ref[after, :], MK)
    right_term[2 * NB :, :] = cross_dot(part, a_ref[across, :], MK)
    full, part = rows(NB + HALF, NB), rows(2 * NB + HALF, HALF)
    left_term[:NB, :] = cross_dot(full, c_ref[:, own])
    left_term[NB : 2 * NB, :] = cross_dot(full, c_ref[:, after])
    left_term[2 * NB :, :] = cross_dot(part, c_ref[:, across])


def sliced_terms(sid, x, a, c):
    size = x.shape[0]
    out = jax.ShapeDtypeStruct((2 * NB + HALF, NB), f32)
    return pl.pallas_call(
        sliced_terms_kernel,
        out_shape=(out, out),
        in_specs=[SMEM] + [VMEM] * 3,
        out_specs=(VMEM, VMEM),
        scratch_shapes=[pltpu.VMEM((3 * NB, size), f32), pltpu.VMEM((NB, size), f32)],
        compiler_params=PARAMS,
        cost_estimate=pl.CostEstimate(flops=4 * size**3, bytes_accessed=16 * size * size, transcendentals=0),
        name="sliced_terms",
    )(sid, x, a, c)


def row_terms_kernel(sid_ref, x_ref, a_ref, c_ref, right_term, left_term):
    col = pl.multiple_of(sid_ref[0] * NB, NB)
    lhs = jnp.concatenate([a_ref[pl.ds(col, NB), :], c_ref[:, pl.ds(col, NB)].T], axis=0)
    z = halves(split_dot(halves(lhs), halves(x_ref[...])))
    right_term[...] = cross_dot((z[0][:NB], z[1][:NB]), a_ref[...], MK).astype(bf16)
    left_term[...] = cross_dot((z[0][NB:], z[1][NB:]), c_ref[...]).astype(bf16)


def row_coupling_kernel(sid_ref, x_ref, a_ref, c_ref, n_ref):
    rows = a_ref[pl.ds(pl.multiple_of(sid_ref[0] * NB, NB), NB), :]
    z = split_dot(halves(rows), halves(x_ref[...]))
    n_ref[...] = cross_dot(halves(z), c_ref[...])


def negate_kernel(n_ref, out_ref):
    out_ref[...] = -n_ref[...]


def cross_dot(a, b, dims=KM):
    if b.dtype == bf16:
        return mm(a[0], b, dims) + mm(a[1], b, dims)
    return split_dot(a, halves(b), dims)


def row_call(kernel, kinds, sid, x, a, c, name):
    size = x.shape[0]
    return pl.pallas_call(
        kernel,
        out_shape=[jax.ShapeDtypeStruct((NB, size), kind) for kind in kinds],
        in_specs=[SMEM] + [VMEM] * 3,
        out_specs=[VMEM] * len(kinds),
        compiler_params=PARAMS,
        cost_estimate=pl.CostEstimate(flops=8 * size**3, bytes_accessed=16 * size * size, transcendentals=0),
        name=name,
    )(sid, x, a, c)


def coupling_kernel(x_ref, a_ref, c_ref, n_ref):
    x = halves(x_ref[...])
    if a_ref.dtype == bf16:
        z = mm(a_ref[...], x[0]) + mm(a_ref[...], x[1])
    else:
        z = split_dot(halves(a_ref[...]), x)
    n_ref[...] = -cross_dot(halves(z), c_ref[...])


def coupled(x, a, c):
    size = x.shape[0]
    return pl.pallas_call(
        coupling_kernel,
        out_shape=jax.ShapeDtypeStruct(x.shape, f32),
        in_specs=[VMEM] * 3,
        out_specs=VMEM,
        compiler_params=PARAMS,
        cost_estimate=pl.CostEstimate(flops=12 * size**3, bytes_accessed=16 * size * size, transcendentals=0),
        name="coupling",
    )(x, a, c)


def passed_along(block, axis, distance, around=False):
    count = lax.axis_size(axis)
    route = [(i, (i + distance) % count) for i in range(count) if around or 0 <= i + distance < count]
    return lax.ppermute(block, axis, route)


def exchanged(blocks):
    return lax.all_to_all(blocks, "swath", 0, 0, tiled=True)


def shards(design, process, prior_prec, routes, counts):
    row_count, size = process.shape[1:]
    swaths = lax.axis_size("swath")
    sid = lax.axis_index("swath")
    total_slots = design.shape[1] * swaths
    sids = sid[None].astype(jnp.int32)
    half = design.shape[1] // 2
    own, ahead = pl.pallas_call(
        functools.partial(weigh_kernel, total_slots),
        out_shape=(
            jax.ShapeDtypeStruct((half, size), bf16),
            jax.ShapeDtypeStruct((half + row_count, size), bf16),
        ),
        in_specs=[SMEM, SMEM, HBM, HBM],
        out_specs=(VMEM, VMEM),
        scratch_shapes=[pltpu.VMEM((design.shape[1], size), bf16), pltpu.VMEM((row_count, size), bf16), pltpu.SemaphoreType.DMA((2,))],
        compiler_params=pltpu.CompilerParams(vmem_limit_bytes=63 * 2**20),
        name="weigh",
    )(counts, routes, design, process)
    incoming = passed_along(ahead, "tm", 1)
    cut = jax.ShapeDtypeStruct((2 * NB + HALF, NB), f32)
    cuts = jax.ShapeDtypeStruct((swaths,) + cut.shape, f32)
    own_gram = pl.pallas_call(
        own_gram_kernel,
        out_shape=jax.ShapeDtypeStruct((size, size), f32),
        in_specs=[VMEM],
        out_specs=VMEM,
        compiler_params=PARAMS,
        cost_estimate=pl.CostEstimate(flops=2 * half * size**2, bytes_accessed=2 * 2**20, transcendentals=0),
        name="own_gram",
    )(own)
    parts, pairs = pl.pallas_call(
        gram_kernel,
        out_shape=(cuts, jax.ShapeDtypeStruct((swaths, 2 * row_count, size), bf16)),
        in_specs=[VMEM] * 3,
        out_specs=(VMEM, VMEM),
        compiler_params=PARAMS,
        name="gram",
    )(own_gram, incoming, process[0])
    diag, copies = pl.pallas_call(
        start_kernel,
        out_shape=(cut, cuts),
        in_specs=[SMEM] + [VMEM] * 4,
        out_specs=(VMEM, VMEM),
        compiler_params=PARAMS,
        name="start",
    )(sids, exchanged(parts), process[0], incoming, prior_prec)
    copies, pairs = lax.optimization_barrier((copies, pairs))
    all_diag = exchanged(copies)
    pairs = exchanged(pairs)
    (x,) = inverse(sids, all_diag)
    a = pairs[:, :row_count].reshape(size, size)
    c = pairs[:, row_count:].reshape(size, size)
    rows = None
    for level in range(LEVELS):
        distance = 2**level
        if level == LEVELS - 1:
            (n,) = row_call(row_coupling_kernel, (f32,), sids, x, a, c, "row_coupling")
            coupling = passed_along(n, "tm", -distance)
            x, n = lax.optimization_barrier((x, n))
            right_term, left_term = row_call(row_terms_kernel, (bf16, bf16), sids, x, a, c, "row_terms")
            from_right = passed_along(right_term, "tm", -distance)
            from_left = passed_along(left_term, "tm", distance)
            coupling = pl.pallas_call(
                negate_kernel,
                out_shape=jax.ShapeDtypeStruct(coupling.shape, f32),
                in_specs=[VMEM],
                out_specs=VMEM,
                compiler_params=PARAMS,
                cost_estimate=pl.CostEstimate(flops=size * NB, bytes_accessed=8 * size * NB, transcendentals=0),
                name="negate",
            )(coupling)
            rows, coupling = lax.optimization_barrier((rows, coupling))
            return ((rows - from_left.astype(f32) - from_right.astype(f32))[None], coupling[None])
        right_term, left_term = sliced_terms(sids, x, a, c)
        x, right_term, left_term = lax.optimization_barrier((x, right_term, left_term))
        from_right = passed_along(right_term, "tm", -distance)
        from_left = passed_along(left_term, "tm", distance)
        n = coupled(x, a, c)
        from_right, from_left, _ = lax.optimization_barrier((from_right, from_left, n))
        diag, copies = pl.pallas_call(
            next_kernel,
            out_shape=(cut, cuts),
            in_specs=[VMEM] * 3,
            out_specs=(VMEM, VMEM),
            compiler_params=PARAMS,
            name="next",
        )(diag, from_left, from_right)
        x, *tail = inverse(sids, exchanged(copies), level == LEVELS - 2)
        rows = tail[0] if tail else None
        a = passed_along(n, "tm", distance)
        c = passed_along(n, "tm", -distance)


def solution(mesh):
    return jax.shard_map(
        shards,
        mesh=mesh,
        in_specs=(
            P("tm", "swath", None),
            P("tm", "swath", None),
            P("tm", "swath"),
            P("tm", "swath"),
            P("tm", "swath"),
        ),
        out_specs=(P("tm", "swath", None), P("tm", "swath", None)),
        check_vma=False,
    )
```

```python
import functools
import jax
import jax.numpy as jnp
from jax import lax
from jax.experimental import pallas as pl
from jax.experimental.pallas import tpu as pltpu
from jax.sharding import PartitionSpec as P

LEVELS = 3
NB = 128
WIDTH = 16
HALF = NB // 2
f32, bf16 = jnp.float32, jnp.bfloat16
VMEM = pl.BlockSpec(memory_space=pltpu.VMEM)
SMEM = pl.BlockSpec(memory_space=pltpu.SMEM)
HBM = pl.BlockSpec(memory_space=pltpu.HBM)
PARAMS = pltpu.CompilerParams(vmem_limit_bytes=48 * 2**20)
KK, KM, MK = ((0,), (0,)), ((1,), (0,)), ((1,), (1,))


def mm(a, b, dims=KM):
    return lax.dot_general(a, b, (dims, ((), ())), preferred_element_type=f32)


def halves(x):
    high = x.astype(bf16)
    return high, (x - high.astype(f32)).astype(bf16)


def thirds(x):
    high = x.astype(bf16).astype(f32)
    rest = x - high
    mid = rest.astype(bf16).astype(f32)
    return high, mid, rest - mid


def split_dot(a, b, dims=KM):
    return mm(a[0], b[0], dims) + (mm(a[0], b[1], dims) + mm(a[1], b[0], dims))


def block_inverse(a):
    lane = lax.broadcasted_iota(jnp.int32, (WIDTH, NB), 1)
    row = lax.broadcasted_iota(jnp.int32, (WIDTH, NB), 0)
    lane_all = lax.broadcasted_iota(jnp.int32, (NB, NB), 1)
    p = a[:WIDTH, :]
    for start in range(0, NB, WIDTH):
        stop = start + WIDTH
        inside = (lane >= start) & (lane < stop)
        cols = [jnp.broadcast_to(p[:, start + j : start + j + 1], (WIDTH, NB)) for j in range(WIDTH)]
        h, m, l = thirds(jnp.where(inside, 0.0, jnp.where(lane < start, -p, p)))
        lhs = jnp.concatenate([h, h, m, h, l, m], axis=0).T.astype(bf16)
        x = jnp.where(inside, jnp.where(lane - start == row, 1.0, 0.0), p)
        if stop < NB:
            after = a[stop : stop + WIDTH, :]
            weights = [jnp.broadcast_to(after[:, start + j : start + j + 1], (WIDTH, NB)) for j in range(WIDTH)]
        units = [1.0 / cols[j][j : j + 1, :] for j in range(WIDTH)]
        scale = jnp.ones((1, NB), f32)
        for j in range(WIDTH):
            c = cols[j]
            now, here = scale * units[j], row == j
            if j + 1 < WIDTH:
                pair = (c[j + 1 : j + 2, :] * units[j + 1]) * (cols[j + 1][j : j + 1, :] * units[j])
                scale = 1.0 / (cols[j + 1][j + 1 : j + 2, :] * units[j + 1] - pair * scale)

            def step(v):
                t = v[j : j + 1, :] * now
                return jnp.where(here, t, v - c * t)

            for i in range(j + 1, WIDTH):
                cols[i] = step(cols[i])
            x = step(x)
        if stop < NB:
            sums = [weights[j] * x[j : j + 1, :] for j in range(4)]
            for j in range(4, WIDTH):
                sums[j % 4] = sums[j % 4] + weights[j] * x[j : j + 1, :]
            p = jnp.where(inside, 0.0, after) - ((sums[0] + sums[1]) + (sums[2] + sums[3]))
        h, m, l = thirds(x)
        rhs = jnp.concatenate([h, m, h, l, h, m], axis=0).astype(bf16)
        a = jnp.where((lane_all >= start) & (lane_all < stop), 0.0, a) - mm(lhs, rhs)
        rows = [x]
        if start:
            rows = [a[:start]] + rows
        if stop < NB:
            rows = rows + [a[stop:]]
        a = jnp.concatenate(rows, axis=0)
    return a


def inverse_kernel(with_rows, sid_ref, g_ref, x_ref, *rest):
    size = x_ref.shape[0]
    count = size // NB
    for k in range(count):
        s, n = slice(k * NB, (k + 1) * NB), (k + 1) % count
        t = slice(n * NB, (n + 1) * NB)
        x_ref[s, s] = g_ref[k, :NB, :]
        block = g_ref[k, NB : 2 * NB, :]
        x_ref[s, t] = block
        x_ref[t, s] = block.T
    for p in range(2):
        s, t = slice(p * NB, (p + 1) * NB), slice((p + 2) * NB, (p + 3) * NB)
        block = jnp.concatenate([g_ref[p, 2 * NB :, :], g_ref[p + 2, 2 * NB :, :]], axis=0)
        x_ref[s, t] = block
        x_ref[t, s] = block.T
    if with_rows:
        rest[0][...] = x_ref[pl.ds(pl.multiple_of(sid_ref[0] * NB, NB), NB), :]
    left_t = rest[-1]
    lane = lax.broadcasted_iota(jnp.int32, (NB, size), 1)

    def eliminate(b, carry):
        first = pl.multiple_of(b * NB, NB)
        at = pl.ds(first, NB)
        inv = block_inverse(x_ref[at, at])
        rows = x_ref[at, :]
        inside = (lane >= first) & (lane < first + NB)
        left_t[...] = jnp.where(lane < first, -rows, rows).T
        w = split_dot(halves(inv), halves(jnp.where(inside, 0.0, rows)))
        w = jnp.where(inside, jnp.concatenate([inv] * count, axis=1), w)
        w_halves = halves(w)
        for i in range(1, count):
            other = pl.ds(pl.multiple_of(lax.rem(b + i, count) * NB, NB), NB)
            x_ref[other, :] = jnp.where(inside, 0.0, x_ref[other, :]) - split_dot(halves(left_t[other, :]), w_halves)
        x_ref[at, :] = w
        return carry

    lax.fori_loop(0, count, eliminate, 0)


def inverse(sid, g, with_rows=False):
    size = 4 * NB
    outs = [jax.ShapeDtypeStruct((size, size), f32)]
    if with_rows:
        outs.append(jax.ShapeDtypeStruct((NB, size), f32))
    return pl.pallas_call(
        functools.partial(inverse_kernel, with_rows),
        out_shape=outs,
        in_specs=[SMEM, VMEM],
        out_specs=[VMEM] * len(outs),
        scratch_shapes=[pltpu.VMEM((size, NB), f32)],
        compiler_params=PARAMS,
        cost_estimate=pl.CostEstimate(flops=40*size**3 if with_rows else 60 * size**3, bytes_accessed=8 * size * size, transcendentals=0),
        name="inverse",
    )(sid, g)


def weigh_kernel(total_slots, counts_ref, routes_ref, design_hbm, process_hbm, own_ref, ahead_ref, design_ref, process_ref, sems):
    rows = own_ref.shape[0] // 2
    loads = [
        pltpu.make_async_copy(design_hbm.at[0], design_ref, sems.at[0]),
        pltpu.make_async_copy(process_hbm.at[0], process_ref, sems.at[1]),
    ]
    for load in loads:
        load.start()
    me, live_count = lax.axis_index("tm"), counts_ref[0, 0]
    loads[0].wait()
    own_seen = jnp.int32(0)
    for r in range(4):
        target = routes_ref[0, r]
        is_own = target == me
        live = (r < live_count) & (is_own | (target == me + 1))
        h = design_ref[r * rows : (r + 1) * rows, :].astype(f32)
        mean_sq = jnp.mean(h * h, axis=-1, keepdims=True)
        w = h * lax.rsqrt(4.0 * total_slots * (mean_sq + 1e-06))
        w = jnp.where(live, w, 0.0).astype(bf16)
        ahead_seen = r - own_seen

        @pl.when(is_own)
        def _():
            own_ref[pl.ds(jnp.minimum(own_seen, 1) * rows, rows), :] = w

        @pl.when(jnp.logical_not(is_own))
        def _():
            ahead_ref[pl.ds(jnp.minimum(ahead_seen, 1) * rows, rows), :] = w

        own_seen = own_seen + jnp.where(is_own, 1, 0)
    loads[1].wait()
    ahead_ref[2 * rows :, :] = process_ref[...]


def own_gram_kernel(own_ref, g_ref):
    g_ref[...] = mm(own_ref[...], own_ref[...], KK)


def gram_kernel(g_ref, incoming_ref, process_ref, out_ref, pairs_ref):
    half = incoming_ref.shape[0] - NB
    g = g_ref[...] + mm(incoming_ref[:half, :], incoming_ref[:half, :], KK)
    for k in range(4):
        n, p, h = (k + 1) % 4, k % 2, HALF * (k // 2)
        out_ref[k, :NB, :] = g[k * NB : (k + 1) * NB, k * NB : (k + 1) * NB]
        out_ref[k, NB : 2 * NB, :] = g[k * NB : (k + 1) * NB, n * NB : (n + 1) * NB]
        pairs_ref[k, :NB, :] = incoming_ref[half:, :]
        pairs_ref[k, NB:, :] = process_ref[...]
        out_ref[k, 2 * NB :, :] = g[p * NB + h : p * NB + h + HALF, (p + 2) * NB : (p + 3) * NB]


def start_kernel(sid_ref, parts_ref, own_ref, incoming_ref, prior_ref, d_ref, copies_ref):
    q = sid_ref[0]
    rows = own_ref[...].astype(f32) + incoming_ref[incoming_ref.shape[0] - NB :, :].astype(f32)
    total = (parts_ref[0] + parts_ref[1]) + (parts_ref[2] + parts_ref[3])

    def block(k):
        out = rows[:, :NB]
        for j in range(1, 4):
            out = jnp.where(k == j, rows[:, j * NB : (j + 1) * NB], out)
        return out

    unit = lax.broadcasted_iota(jnp.int32, (NB, NB), 0) == lax.broadcasted_iota(jnp.int32, (NB, NB), 1)
    across = block(lax.rem(q + 2, 4))
    half = jnp.where(q < 2, across[:HALF, :], across.T[HALF:, :])
    d = jnp.concatenate(
        [
            total[:NB] + (block(q) + jnp.where(unit, prior_ref[...], 0.0)),
            total[NB : 2 * NB] + block(lax.rem(q + 1, 4)),
            total[2 * NB :] + half,
        ],
        axis=0,
    )
    d_ref[...] = d
    for k in range(4):
        copies_ref[k] = d


def next_kernel(d_in, left_ref, right_ref, d_ref, copies_ref):
    d = d_in[...] - left_ref[...] - right_ref[...]
    d_ref[...] = d
    for k in range(4):
        copies_ref[k] = d


def sliced_terms_kernel(sid_ref, x_ref, a_ref, c_ref, right_term, left_term, lhs, flipped):
    q = sid_ref[0]
    p, h = lax.rem(q, 2), pl.multiple_of(lax.div(q, 2) * HALF, HALF)

    def at(k):
        return pl.ds(pl.multiple_of(k * NB, NB), NB)

    own, after, across = at(q), at(lax.rem(q + 1, 4)), at(p + 2)
    lhs[:NB, :] = a_ref[own, :].astype(f32)
    lhs[NB : NB + HALF, :] = a_ref[pl.ds(pl.multiple_of(p * NB + h, HALF), HALF), :].astype(f32)
    lhs[NB + HALF : 2 * NB + HALF, :] = c_ref[:, own].astype(f32).T
    flipped[...] = c_ref[:, at(p)].astype(f32).T
    lhs[2 * NB + HALF :, :] = flipped[pl.ds(h, HALF), :]
    z = halves(split_dot(halves(lhs[...]), halves(x_ref[...])))

    def rows(first, count):
        return z[0][first : first + count], z[1][first : first + count]

    full, part = rows(0, NB), rows(NB, HALF)
    right_term[:NB, :] = cross_dot(full, a_ref[own, :], MK)
    right_term[NB : 2 * NB, :] = cross_dot(full, a_ref[after, :], MK)
    right_term[2 * NB :, :] = cross_dot(part, a_ref[across, :], MK)
    full, part = rows(NB + HALF, NB), rows(2 * NB + HALF, HALF)
    left_term[:NB, :] = cross_dot(full, c_ref[:, own])
    left_term[NB : 2 * NB, :] = cross_dot(full, c_ref[:, after])
    left_term[2 * NB :, :] = cross_dot(part, c_ref[:, across])


def sliced_terms(sid, x, a, c):
    size = x.shape[0]
    out = jax.ShapeDtypeStruct((2 * NB + HALF, NB), f32)
    return pl.pallas_call(
        sliced_terms_kernel,
        out_shape=(out, out),
        in_specs=[SMEM] + [VMEM] * 3,
        out_specs=(VMEM, VMEM),
        scratch_shapes=[pltpu.VMEM((3 * NB, size), f32), pltpu.VMEM((NB, size), f32)],
        compiler_params=PARAMS,
        cost_estimate=pl.CostEstimate(flops=4 * size**3, bytes_accessed=16 * size * size, transcendentals=0),
        name="sliced_terms",
    )(sid, x, a, c)


def row_terms_kernel(sid_ref, x_ref, a_ref, c_ref, right_term, left_term):
    col = pl.multiple_of(sid_ref[0] * NB, NB)
    lhs = jnp.concatenate([a_ref[pl.ds(col, NB), :], c_ref[:, pl.ds(col, NB)].T], axis=0)
    z = halves(split_dot(halves(lhs), halves(x_ref[...])))
    right_term[...] = cross_dot((z[0][:NB], z[1][:NB]), a_ref[...], MK)
    left_term[...] = cross_dot((z[0][NB:], z[1][NB:]), c_ref[...])


def row_coupling_kernel(sid_ref, x_ref, a_ref, c_ref, n_ref):
    rows = a_ref[pl.ds(pl.multiple_of(sid_ref[0] * NB, NB), NB), :]
    z = split_dot(halves(rows), halves(x_ref[...]))
    n_ref[...] = cross_dot(halves(z), c_ref[...])


def negate_kernel(n_ref, out_ref):
    out_ref[...] = -n_ref[...]


def cross_dot(a, b, dims=KM):
    if b.dtype == bf16:
        return mm(a[0], b, dims) + mm(a[1], b, dims)
    return split_dot(a, halves(b), dims)


def row_call(kernel, kinds, sid, x, a, c, name):
    size = x.shape[0]
    return pl.pallas_call(
        kernel,
        out_shape=[jax.ShapeDtypeStruct((NB, size), kind) for kind in kinds],
        in_specs=[SMEM] + [VMEM] * 3,
        out_specs=[VMEM] * len(kinds),
        compiler_params=PARAMS,
        cost_estimate=pl.CostEstimate(flops=8 * size**3, bytes_accessed=16 * size * size, transcendentals=0),
        name=name,
    )(sid, x, a, c)


def coupling_kernel(x_ref, a_ref, c_ref, n_ref):
    x = halves(x_ref[...])
    if a_ref.dtype == bf16:
        z = mm(a_ref[...], x[0]) + mm(a_ref[...], x[1])
    else:
        z = split_dot(halves(a_ref[...]), x)
    n_ref[...] = -cross_dot(halves(z), c_ref[...])


def coupled(x, a, c):
    size = x.shape[0]
    return pl.pallas_call(
        coupling_kernel,
        out_shape=jax.ShapeDtypeStruct(x.shape, f32),
        in_specs=[VMEM] * 3,
        out_specs=VMEM,
        compiler_params=PARAMS,
        cost_estimate=pl.CostEstimate(flops=12 * size**3, bytes_accessed=16 * size * size, transcendentals=0),
        name="coupling",
    )(x, a, c)


def passed_along(block, axis, distance, around=False):
    count = lax.axis_size(axis)
    route = [(i, (i + distance) % count) for i in range(count) if around or 0 <= i + distance < count]
    return lax.ppermute(block, axis, route)


def exchanged(blocks):
    return lax.all_to_all(blocks, "swath", 0, 0, tiled=True)


def shards(design, process, prior_prec, routes, counts):
    row_count, size = process.shape[1:]
    swaths = lax.axis_size("swath")
    sid = lax.axis_index("swath")
    total_slots = design.shape[1] * swaths
    sids = sid[None].astype(jnp.int32)
    half = design.shape[1] // 2
    own, ahead = pl.pallas_call(
        functools.partial(weigh_kernel, total_slots),
        out_shape=(
            jax.ShapeDtypeStruct((half, size), bf16),
            jax.ShapeDtypeStruct((half + row_count, size), bf16),
        ),
        in_specs=[SMEM, SMEM, HBM, HBM],
        out_specs=(VMEM, VMEM),
        scratch_shapes=[pltpu.VMEM((design.shape[1], size), bf16), pltpu.VMEM((row_count, size), bf16), pltpu.SemaphoreType.DMA((2,))],
        compiler_params=pltpu.CompilerParams(vmem_limit_bytes=63 * 2**20),
        name="weigh",
    )(counts, routes, design, process)
    incoming = passed_along(ahead, "tm", 1)
    cut = jax.ShapeDtypeStruct((2 * NB + HALF, NB), f32)
    cuts = jax.ShapeDtypeStruct((swaths,) + cut.shape, f32)
    own_gram = pl.pallas_call(
        own_gram_kernel,
        out_shape=jax.ShapeDtypeStruct((size, size), f32),
        in_specs=[VMEM],
        out_specs=VMEM,
        compiler_params=PARAMS,
        cost_estimate=pl.CostEstimate(flops=2 * half * size**2, bytes_accessed=2 * 2**20, transcendentals=0),
        name="own_gram",
    )(own)
    parts, pairs = pl.pallas_call(
        gram_kernel,
        out_shape=(cuts, jax.ShapeDtypeStruct((swaths, 2 * row_count, size), bf16)),
        in_specs=[VMEM] * 3,
        out_specs=(VMEM, VMEM),
        compiler_params=PARAMS,
        name="gram",
    )(own_gram, incoming, process[0])
    diag, copies = pl.pallas_call(
        start_kernel,
        out_shape=(cut, cuts),
        in_specs=[SMEM] + [VMEM] * 4,
        out_specs=(VMEM, VMEM),
        compiler_params=PARAMS,
        name="start",
    )(sids, exchanged(parts), process[0], incoming, prior_prec)
    copies, pairs = lax.optimization_barrier((copies, pairs))
    all_diag = exchanged(copies)
    pairs = exchanged(pairs)
    (x,) = inverse(sids, all_diag)
    a = pairs[:, :row_count].reshape(size, size)
    c = pairs[:, row_count:].reshape(size, size)
    rows = None
    for level in range(LEVELS):
        distance = 2**level
        if level == LEVELS - 1:
            (n,) = row_call(row_coupling_kernel, (f32,), sids, x, a, c, "row_coupling")
            coupling = passed_along(n, "tm", -distance)
            x, n = lax.optimization_barrier((x, n))
            right_term, left_term = row_call(row_terms_kernel, (f32, f32), sids, x, a, c, "row_terms")
            from_right = passed_along(right_term, "tm", -distance)
            from_left = passed_along(left_term, "tm", distance)
            coupling = pl.pallas_call(
                negate_kernel,
                out_shape=jax.ShapeDtypeStruct(coupling.shape, f32),
                in_specs=[VMEM],
                out_specs=VMEM,
                compiler_params=PARAMS,
                cost_estimate=pl.CostEstimate(flops=size * NB, bytes_accessed=8 * size * NB, transcendentals=0),
                name="negate",
            )(coupling)
            rows, coupling = lax.optimization_barrier((rows, coupling))
            return ((rows - from_left - from_right)[None], coupling[None])
        right_term, left_term = sliced_terms(sids, x, a, c)
        x, right_term, left_term = lax.optimization_barrier((x, right_term, left_term))
        from_right = passed_along(right_term, "tm", -distance)
        from_left = passed_along(left_term, "tm", distance)
        n = coupled(x, a, c)
        from_right, from_left, _ = lax.optimization_barrier((from_right, from_left, n))
        diag, copies = pl.pallas_call(
            next_kernel,
            out_shape=(cut, cuts),
            in_specs=[VMEM] * 3,
            out_specs=(VMEM, VMEM),
            compiler_params=PARAMS,
            name="next",
        )(diag, from_left, from_right)
        x, *tail = inverse(sids, exchanged(copies), level == LEVELS - 2)
        rows = tail[0] if tail else None
        a = passed_along(n, "tm", distance)
        c = passed_along(n, "tm", -distance)


def solution(mesh):
    return jax.shard_map(
        shards,
        mesh=mesh,
        in_specs=(
            P("tm", "swath", None),
            P("tm", "swath", None),
            P("tm", "swath"),
            P("tm", "swath"),
            P("tm", "swath"),
        ),
        out_specs=(P("tm", "swath", None), P("tm", "swath", None)),
        check_vma=False,
    )
```

```python
import functools
import jax
import jax.numpy as jnp
from jax import lax
from jax.experimental import pallas as pl
from jax.experimental.pallas import tpu as pltpu
from jax.sharding import PartitionSpec as P

LEVELS = 3
NB = 128
WIDTH = 16
HALF = NB // 2
f32, bf16 = jnp.float32, jnp.bfloat16
VMEM = pl.BlockSpec(memory_space=pltpu.VMEM)
SMEM = pl.BlockSpec(memory_space=pltpu.SMEM)
HBM = pl.BlockSpec(memory_space=pltpu.HBM)
PARAMS = pltpu.CompilerParams(vmem_limit_bytes=48 * 2**20)
KK, KM, MK = ((0,), (0,)), ((1,), (0,)), ((1,), (1,))


def mm(a, b, dims=KM):
    return lax.dot_general(a, b, (dims, ((), ())), preferred_element_type=f32)


def halves(x):
    high = x.astype(bf16)
    return high, (x - high.astype(f32)).astype(bf16)


def thirds(x):
    high = x.astype(bf16).astype(f32)
    rest = x - high
    mid = rest.astype(bf16).astype(f32)
    return high, mid, rest - mid


def split_dot(a, b, dims=KM):
    return mm(a[0], b[0], dims) + (mm(a[0], b[1], dims) + mm(a[1], b[0], dims))


def block_inverse(a):
    lane = lax.broadcasted_iota(jnp.int32, (WIDTH, NB), 1)
    row = lax.broadcasted_iota(jnp.int32, (WIDTH, NB), 0)
    lane_all = lax.broadcasted_iota(jnp.int32, (NB, NB), 1)
    p = a[:WIDTH, :]
    for start in range(0, NB, WIDTH):
        stop = start + WIDTH
        inside = (lane >= start) & (lane < stop)
        cols = [jnp.broadcast_to(p[:, start + j : start + j + 1], (WIDTH, NB)) for j in range(WIDTH)]
        h, m, l = thirds(jnp.where(inside, 0.0, jnp.where(lane < start, -p, p)))
        lhs = jnp.concatenate([h, h, m, h, l, m], axis=0).T.astype(bf16)
        x = jnp.where(inside, jnp.where(lane - start == row, 1.0, 0.0), p)
        if stop < NB:
            after = a[stop : stop + WIDTH, :]
            weights = [jnp.broadcast_to(after[:, start + j : start + j + 1], (WIDTH, NB)) for j in range(WIDTH)]
        units = [1.0 / cols[j][j : j + 1, :] for j in range(WIDTH)]
        scale = jnp.ones((1, NB), f32)
        for j in range(WIDTH):
            c = cols[j]
            now, here = scale * units[j], row == j
            if j + 1 < WIDTH:
                pair = (c[j + 1 : j + 2, :] * units[j + 1]) * (cols[j + 1][j : j + 1, :] * units[j])
                scale = 1.0 / (cols[j + 1][j + 1 : j + 2, :] * units[j + 1] - pair * scale)

            def step(v):
                t = v[j : j + 1, :] * now
                return jnp.where(here, t, v - c * t)

            for i in range(j + 1, WIDTH):
                cols[i] = step(cols[i])
            x = step(x)
        if stop < NB:
            sums = [weights[j] * x[j : j + 1, :] for j in range(4)]
            for j in range(4, WIDTH):
                sums[j % 4] = sums[j % 4] + weights[j] * x[j : j + 1, :]
            p = jnp.where(inside, 0.0, after) - ((sums[0] + sums[1]) + (sums[2] + sums[3]))
        h, m, l = thirds(x)
        rhs = jnp.concatenate([h, m, h, l, h, m], axis=0).astype(bf16)
        a = jnp.where((lane_all >= start) & (lane_all < stop), 0.0, a) - mm(lhs, rhs)
        rows = [x]
        if start:
            rows = [a[:start]] + rows
        if stop < NB:
            rows = rows + [a[stop:]]
        a = jnp.concatenate(rows, axis=0)
    return a


def inverse_kernel(with_rows, sid_ref, g_ref, x_ref, *rest):
    size = x_ref.shape[0]
    count = size // NB
    for k in range(count):
        s, n = slice(k * NB, (k + 1) * NB), (k + 1) % count
        t = slice(n * NB, (n + 1) * NB)
        x_ref[s, s] = g_ref[k, :NB, :]
        block = g_ref[k, NB : 2 * NB, :]
        x_ref[s, t] = block
        x_ref[t, s] = block.T
    for p in range(2):
        s, t = slice(p * NB, (p + 1) * NB), slice((p + 2) * NB, (p + 3) * NB)
        block = jnp.concatenate([g_ref[p, 2 * NB :, :], g_ref[p + 2, 2 * NB :, :]], axis=0)
        x_ref[s, t] = block
        x_ref[t, s] = block.T
    if with_rows:
        rest[0][...] = x_ref[pl.ds(pl.multiple_of(sid_ref[0] * NB, NB), NB), :]
    left_t = rest[-1]
    lane = lax.broadcasted_iota(jnp.int32, (NB, size), 1)

    def eliminate(b, carry):
        first = pl.multiple_of(b * NB, NB)
        at = pl.ds(first, NB)
        inv = block_inverse(x_ref[at, at])
        rows = x_ref[at, :]
        inside = (lane >= first) & (lane < first + NB)
        left_t[...] = jnp.where(lane < first, -rows, rows).T
        w = split_dot(halves(inv), halves(jnp.where(inside, 0.0, rows)))
        w = jnp.where(inside, jnp.concatenate([inv] * count, axis=1), w)
        w_halves = halves(w)
        for i in range(1, count):
            other = pl.ds(pl.multiple_of(lax.rem(b + i, count) * NB, NB), NB)
            x_ref[other, :] = jnp.where(inside, 0.0, x_ref[other, :]) - split_dot(halves(left_t[other, :]), w_halves)
        x_ref[at, :] = w
        return carry

    lax.fori_loop(0, count, eliminate, 0)


def inverse(sid, g, with_rows=False):
    size = 4 * NB
    outs = [jax.ShapeDtypeStruct((size, size), f32)]
    if with_rows:
        outs.append(jax.ShapeDtypeStruct((NB, size), f32))
    return pl.pallas_call(
        functools.partial(inverse_kernel, with_rows),
        out_shape=outs,
        in_specs=[SMEM, VMEM],
        out_specs=[VMEM] * len(outs),
        scratch_shapes=[pltpu.VMEM((size, NB), f32)],
        compiler_params=PARAMS,
        cost_estimate=pl.CostEstimate(flops=40 * size**3, bytes_accessed=8 * size * size, transcendentals=0),
        name="inverse",
    )(sid, g)


def weigh_kernel(total_slots, counts_ref, routes_ref, design_hbm, process_hbm, own_ref, ahead_ref, design_ref, process_ref, sems):
    rows = own_ref.shape[0] // 2
    loads = [
        pltpu.make_async_copy(design_hbm.at[0], design_ref, sems.at[0]),
        pltpu.make_async_copy(process_hbm.at[0], process_ref, sems.at[1]),
    ]
    for load in loads:
        load.start()
    me, live_count = lax.axis_index("tm"), counts_ref[0, 0]
    loads[0].wait()
    own_seen = jnp.int32(0)
    for r in range(4):
        target = routes_ref[0, r]
        is_own = target == me
        live = (r < live_count) & (is_own | (target == me + 1))
        h = design_ref[r * rows : (r + 1) * rows, :].astype(f32)
        mean_sq = jnp.mean(h * h, axis=-1, keepdims=True)
        w = h * lax.rsqrt(4.0 * total_slots * (mean_sq + 1e-06))
        w = jnp.where(live, w, 0.0).astype(bf16)
        ahead_seen = r - own_seen

        @pl.when(is_own)
        def _():
            own_ref[pl.ds(jnp.minimum(own_seen, 1) * rows, rows), :] = w

        @pl.when(jnp.logical_not(is_own))
        def _():
            ahead_ref[pl.ds(jnp.minimum(ahead_seen, 1) * rows, rows), :] = w

        own_seen = own_seen + jnp.where(is_own, 1, 0)
    loads[1].wait()
    ahead_ref[2 * rows :, :] = process_ref[...]


def own_gram_kernel(own_ref, g_ref):
    g_ref[...] = mm(own_ref[...], own_ref[...], KK)


def gram_kernel(g_ref, incoming_ref, process_ref, out_ref, pairs_ref):
    half = incoming_ref.shape[0] - NB
    g = g_ref[...] + mm(incoming_ref[:half, :], incoming_ref[:half, :], KK)
    for k in range(4):
        n, p, h = (k + 1) % 4, k % 2, HALF * (k // 2)
        out_ref[k, :NB, :] = g[k * NB : (k + 1) * NB, k * NB : (k + 1) * NB]
        out_ref[k, NB : 2 * NB, :] = g[k * NB : (k + 1) * NB, n * NB : (n + 1) * NB]
        pairs_ref[k, :NB, :] = incoming_ref[half:, :]
        pairs_ref[k, NB:, :] = process_ref[...]
        out_ref[k, 2 * NB :, :] = g[p * NB + h : p * NB + h + HALF, (p + 2) * NB : (p + 3) * NB]


def start_kernel(sid_ref, parts_ref, own_ref, incoming_ref, prior_ref, d_ref, copies_ref):
    q = sid_ref[0]
    rows = own_ref[...].astype(f32) + incoming_ref[incoming_ref.shape[0] - NB :, :].astype(f32)
    total = (parts_ref[0] + parts_ref[1]) + (parts_ref[2] + parts_ref[3])

    def block(k):
        out = rows[:, :NB]
        for j in range(1, 4):
            out = jnp.where(k == j, rows[:, j * NB : (j + 1) * NB], out)
        return out

    unit = lax.broadcasted_iota(jnp.int32, (NB, NB), 0) == lax.broadcasted_iota(jnp.int32, (NB, NB), 1)
    across = block(lax.rem(q + 2, 4))
    half = jnp.where(q < 2, across[:HALF, :], across.T[HALF:, :])
    d = jnp.concatenate(
        [
            total[:NB] + (block(q) + jnp.where(unit, prior_ref[...], 0.0)),
            total[NB : 2 * NB] + block(lax.rem(q + 1, 4)),
            total[2 * NB :] + half,
        ],
        axis=0,
    )
    d_ref[...] = d
    for k in range(4):
        copies_ref[k] = d


def next_kernel(d_in, left_ref, right_ref, d_ref, copies_ref):
    d = d_in[...] - left_ref[...] - right_ref[...]
    d_ref[...] = d
    for k in range(4):
        copies_ref[k] = d


def sliced_terms_kernel(sid_ref, x_ref, a_ref, c_ref, right_term, left_term, lhs, flipped):
    q = sid_ref[0]
    p, h = lax.rem(q, 2), pl.multiple_of(lax.div(q, 2) * HALF, HALF)

    def at(k):
        return pl.ds(pl.multiple_of(k * NB, NB), NB)

    own, after, across = at(q), at(lax.rem(q + 1, 4)), at(p + 2)
    lhs[:NB, :] = a_ref[own, :].astype(f32)
    lhs[NB : NB + HALF, :] = a_ref[pl.ds(pl.multiple_of(p * NB + h, HALF), HALF), :].astype(f32)
    lhs[NB + HALF : 2 * NB + HALF, :] = c_ref[:, own].astype(f32).T
    flipped[...] = c_ref[:, at(p)].astype(f32).T
    lhs[2 * NB + HALF :, :] = flipped[pl.ds(h, HALF), :]
    z = halves(split_dot(halves(lhs[...]), halves(x_ref[...])))

    def rows(first, count):
        return z[0][first : first + count], z[1][first : first + count]

    full, part = rows(0, NB), rows(NB, HALF)
    right_term[:NB, :] = cross_dot(full, a_ref[own, :], MK)
    right_term[NB : 2 * NB, :] = cross_dot(full, a_ref[after, :], MK)
    right_term[2 * NB :, :] = cross_dot(part, a_ref[across, :], MK)
    full, part = rows(NB + HALF, NB), rows(2 * NB + HALF, HALF)
    left_term[:NB, :] = cross_dot(full, c_ref[:, own])
    left_term[NB : 2 * NB, :] = cross_dot(full, c_ref[:, after])
    left_term[2 * NB :, :] = cross_dot(part, c_ref[:, across])


def sliced_terms(sid, x, a, c):
    size = x.shape[0]
    out = jax.ShapeDtypeStruct((2 * NB + HALF, NB), f32)
    return pl.pallas_call(
        sliced_terms_kernel,
        out_shape=(out, out),
        in_specs=[SMEM] + [VMEM] * 3,
        out_specs=(VMEM, VMEM),
        scratch_shapes=[pltpu.VMEM((3 * NB, size), f32), pltpu.VMEM((NB, size), f32)],
        compiler_params=PARAMS,
        cost_estimate=pl.CostEstimate(flops=4 * size**3, bytes_accessed=16 * size * size, transcendentals=0),
        name="sliced_terms",
    )(sid, x, a, c)


def row_terms_kernel(sid_ref, x_ref, a_ref, c_ref, right_term, left_term):
    col = pl.multiple_of(sid_ref[0] * NB, NB)
    lhs = jnp.concatenate([a_ref[pl.ds(col, NB), :], c_ref[:, pl.ds(col, NB)].T], axis=0)
    z = halves(split_dot(halves(lhs), halves(x_ref[...])))
    right_term[...] = cross_dot((z[0][:NB], z[1][:NB]), a_ref[...], MK)
    left_term[...] = cross_dot((z[0][NB:], z[1][NB:]), c_ref[...])


def row_coupling_kernel(sid_ref, x_ref, a_ref, c_ref, n_ref):
    rows = a_ref[pl.ds(pl.multiple_of(sid_ref[0] * NB, NB), NB), :]
    z = split_dot(halves(rows), halves(x_ref[...]))
    n_ref[...] = cross_dot(halves(z), c_ref[...])


def negate_kernel(n_ref, out_ref):
    out_ref[...] = -n_ref[...]


def cross_dot(a, b, dims=KM):
    if b.dtype == bf16:
        return mm(a[0], b, dims) + mm(a[1], b, dims)
    return split_dot(a, halves(b), dims)


def row_call(kernel, kinds, sid, x, a, c, name):
    size = x.shape[0]
    return pl.pallas_call(
        kernel,
        out_shape=[jax.ShapeDtypeStruct((NB, size), kind) for kind in kinds],
        in_specs=[SMEM] + [VMEM] * 3,
        out_specs=[VMEM] * len(kinds),
        compiler_params=PARAMS,
        cost_estimate=pl.CostEstimate(flops=8 * size**3, bytes_accessed=16 * size * size, transcendentals=0),
        name=name,
    )(sid, x, a, c)


def coupling_kernel(x_ref, a_ref, c_ref, n_ref):
    x = halves(x_ref[...])
    if a_ref.dtype == bf16:
        z = mm(a_ref[...], x[0]) + mm(a_ref[...], x[1])
    else:
        z = split_dot(halves(a_ref[...]), x)
    n_ref[...] = -cross_dot(halves(z), c_ref[...])


def coupled(x, a, c):
    size = x.shape[0]
    return pl.pallas_call(
        coupling_kernel,
        out_shape=jax.ShapeDtypeStruct(x.shape, f32),
        in_specs=[VMEM] * 3,
        out_specs=VMEM,
        compiler_params=PARAMS,
        cost_estimate=pl.CostEstimate(flops=12 * size**3, bytes_accessed=16 * size * size, transcendentals=0),
        name="coupling",
    )(x, a, c)


def passed_along(block, axis, distance, around=False):
    count = lax.axis_size(axis)
    route = [(i, (i + distance) % count) for i in range(count) if around or 0 <= i + distance < count]
    return lax.ppermute(block, axis, route)


def exchanged(blocks):
    return lax.all_to_all(blocks, "swath", 0, 0, tiled=True)


def shards(design, process, prior_prec, routes, counts):
    row_count, size = process.shape[1:]
    swaths = lax.axis_size("swath")
    sid = lax.axis_index("swath")
    total_slots = design.shape[1] * swaths
    sids = sid[None].astype(jnp.int32)
    half = design.shape[1] // 2
    own, ahead = pl.pallas_call(
        functools.partial(weigh_kernel, total_slots),
        out_shape=(
            jax.ShapeDtypeStruct((half, size), bf16),
            jax.ShapeDtypeStruct((half + row_count, size), bf16),
        ),
        in_specs=[SMEM, SMEM, HBM, HBM],
        out_specs=(VMEM, VMEM),
        scratch_shapes=[pltpu.VMEM((design.shape[1], size), bf16), pltpu.VMEM((row_count, size), bf16), pltpu.SemaphoreType.DMA((2,))],
        compiler_params=pltpu.CompilerParams(vmem_limit_bytes=63 * 2**20),
        name="weigh",
    )(counts, routes, design, process)
    incoming = passed_along(ahead, "tm", 1)
    cut = jax.ShapeDtypeStruct((2 * NB + HALF, NB), f32)
    cuts = jax.ShapeDtypeStruct((swaths,) + cut.shape, f32)
    own_gram = pl.pallas_call(
        own_gram_kernel,
        out_shape=jax.ShapeDtypeStruct((size, size), f32),
        in_specs=[VMEM],
        out_specs=VMEM,
        compiler_params=PARAMS,
        cost_estimate=pl.CostEstimate(flops=2 * half * size**2, bytes_accessed=2 * 2**20, transcendentals=0),
        name="own_gram",
    )(own)
    parts, pairs = pl.pallas_call(
        gram_kernel,
        out_shape=(cuts, jax.ShapeDtypeStruct((swaths, 2 * row_count, size), bf16)),
        in_specs=[VMEM] * 3,
        out_specs=(VMEM, VMEM),
        compiler_params=PARAMS,
        name="gram",
    )(own_gram, incoming, process[0])
    diag, copies = pl.pallas_call(
        start_kernel,
        out_shape=(cut, cuts),
        in_specs=[SMEM] + [VMEM] * 4,
        out_specs=(VMEM, VMEM),
        compiler_params=PARAMS,
        name="start",
    )(sids, exchanged(parts), process[0], incoming, prior_prec)
    copies, pairs = lax.optimization_barrier((copies, pairs))
    all_diag = exchanged(copies)
    pairs = exchanged(pairs)
    (x,) = inverse(sids, all_diag)
    a = pairs[:, :row_count].reshape(size, size)
    c = pairs[:, row_count:].reshape(size, size)
    rows = None
    for level in range(LEVELS):
        distance = 2**level
        if level == LEVELS - 1:
            (n,) = row_call(row_coupling_kernel, (f32,), sids, x, a, c, "row_coupling")
            coupling = passed_along(n, "tm", -distance)
            x, n = lax.optimization_barrier((x, n))
            right_term, left_term = row_call(row_terms_kernel, (f32, f32), sids, x, a, c, "row_terms")
            from_right = passed_along(right_term, "tm", -distance)
            from_left = passed_along(left_term, "tm", distance)
            coupling = pl.pallas_call(
                negate_kernel,
                out_shape=jax.ShapeDtypeStruct(coupling.shape, f32),
                in_specs=[VMEM],
                out_specs=VMEM,
                compiler_params=PARAMS,
                cost_estimate=pl.CostEstimate(flops=size * NB, bytes_accessed=8 * size * NB, transcendentals=0),
                name="negate",
            )(coupling)
            rows, coupling = lax.optimization_barrier((rows, coupling))
            return ((rows - from_left - from_right)[None], coupling[None])
        right_term, left_term = sliced_terms(sids, x, a, c)
        x, right_term, left_term = lax.optimization_barrier((x, right_term, left_term))
        from_right = passed_along(right_term, "tm", -distance)
        from_left = passed_along(left_term, "tm", distance)
        n = coupled(x, a, c)
        from_right, from_left, _ = lax.optimization_barrier((from_right, from_left, n))
        diag, copies = pl.pallas_call(
            next_kernel,
            out_shape=(cut, cuts),
            in_specs=[VMEM] * 3,
            out_specs=(VMEM, VMEM),
            compiler_params=PARAMS,
            name="next",
        )(diag, from_left, from_right)
        x, *tail = inverse(sids, exchanged(copies), level == LEVELS - 2)
        rows = tail[0] if tail else None
        a = passed_along(n, "tm", distance)
        c = passed_along(n, "tm", -distance)


def solution(mesh):
    return jax.shard_map(
        shards,
        mesh=mesh,
        in_specs=(
            P("tm", "swath", None),
            P("tm", "swath", None),
            P("tm", "swath"),
            P("tm", "swath"),
            P("tm", "swath"),
        ),
        out_specs=(P("tm", "swath", None), P("tm", "swath", None)),
        check_vma=False,
    )
```
